256 devices in a mesh: lev: 8 (over y, core), wave: 32 (over z, x).
Axes of the slice: x: 4, y: 4, z: 8, core: 2. Of those that a mesh axis runs over, the one named last changes fastest.
Arguments:
- state: float32 [256, 2, 8, 2, 32, 256], P('wave', None, None, None, 'lev'), may hold values from -6 to 6
- wave_table: int32 [256], replicated, may hold values from 0 to 255, as said below
- lat_table: int32 [384], replicated, may hold values from 0 to 383, as said below
- lat_weight: float32 [384], replicated, may hold values from 0.5 to 2
- legendre: bfloat16 [256, 384, 256], P('wave'), may hold values from -0.375 to 0.375
- w_in: bfloat16 [64, 512], replicated, may hold values from -0.75 to 0.75
- b_in: float32 [512], replicated, may hold values from -3 to 3
- w_lat: float32 [512], replicated, may hold values from -4 to 4
- w_mid: bfloat16 [512, 512], replicated, may hold values from -0.25 to 0.25
- b_mid: float32 [512], replicated, may hold values from -3 to 3
- w_out: bfloat16 [512, 64], replicated, may hold values from -0.25 to 0.25
- target: float32 [32], P('lev'), may hold values from -4 to 4
- coupling: float32 [256, 32, 32], replicated, may hold values from -1 to 1
Outputs:
- new_state: float32 [256, 2, 8, 2, 32, 256], P('wave', None, None, None, 'lev')
- grid_tend: bfloat16 [8, 64, 384, 768], P('lev', None, 'wave')
The draws below stay inside these ranges and needn't reach their ends.
Inputs may be any that keep to these rules, and one draw needn't show every extreme that they name: `wave_table`: a permutation in which slots 2k and 2k+1 hold a wavenumber m and 255-m. `lat_table`: a permutation in which slots 2k and 2k+1 hold a latitude i and 383-i.
All inputs are finite; a program needn't handle non-finite values.
Results may differ from the reference program's by a relative error of at most 0.0075.
Values may be sent and summed in bfloat16 or wider, within the bound.
No kernel may reach another device: no remote copies, remote signals or barrier semaphores. Data moves between devices by JAX's collectives and lax.ppermute only.
A program may use at most 128 MiB of HBM per device.

```python
import math
import jax
import jax.numpy as jnp
from jax import lax

ENS = 8
FIELDS = 2
LEVELS = 32
MW = 256
NTOT = 256
NLAT = 384
NLON = 768
HID = 512


def draw_wave_table(key, part):
    key = jax.random.fold_in(key, 11)
    lower = jax.random.permutation(key, MW // 2).astype(jnp.int32)
    return jnp.stack([lower, MW - 1 - lower], axis=1).reshape(MW)


def draw_lat_table(key, part):
    key = jax.random.fold_in(key, 23)
    lower = jax.random.permutation(key, NLAT // 2).astype(jnp.int32)
    return jnp.stack([lower, NLAT - 1 - lower], axis=1).reshape(NLAT)


def steps_of(rng, dims, pieces, low, largest):
    def one(axis_at, parts):
        steps = jax.random.uniform(jax.random.fold_in(jax.random.fold_in(rng, 6), axis_at), (parts,), jnp.float32, low / len(pieces), largest / len(pieces))
        return jnp.repeat(jnp.exp(steps), dims[axis_at] // parts).reshape((-1,) + (1,) * (len(dims) - axis_at - 1))

    gain = one(*pieces[0])
    for cut in pieces[1:]:
        gain = gain * one(*cut)
    return gain


def normal_values(key, dims, spread, most, shards=(), kind=jnp.bfloat16):
    factor_of = steps_of(key, dims, shards, -0.22, 0.18) if shards else 1.0
    entries = jax.random.normal(key, dims, jnp.float32) * spread * factor_of
    return jnp.minimum(jnp.maximum(entries, -most), most).astype(kind)


def setup_inputs(seed: int = 0) -> dict:
    seeds = jax.random.split(jax.random.key(seed), 14)
    state = normal_values(seeds[0], (MW, 2, ENS, FIELDS, LEVELS, NTOT), 1.0, 6.0, ((0, 32), (4, 8)), jnp.float32)
    wave_table = draw_wave_table(jax.random.fold_in(seeds[13], 71), 0)
    lat_table = draw_lat_table(jax.random.fold_in(seeds[13], 71), 0)
    lat_weight = jnp.clip(jnp.exp(jax.random.uniform(seeds[3], (NLAT,), jnp.float32, math.log(0.5), math.log(2.0))), 0.5, 2.0)
    legendre = normal_values(seeds[4], (MW, NLAT, NTOT), NTOT ** -0.5, 0.375, ((0, 32),))
    w_in = normal_values(seeds[5], (FIELDS * LEVELS, HID), (FIELDS * LEVELS) ** -0.5, 0.75)
    b_in = normal_values(seeds[6], (HID,), 0.5, 3.0, (), jnp.float32)
    w_lat = normal_values(seeds[7], (HID,), 1.0, 4.0, (), jnp.float32)
    w_mid = normal_values(seeds[8], (HID, HID), HID ** -0.5, 0.25)
    b_mid = normal_values(seeds[9], (HID,), 0.5, 3.0, (), jnp.float32)
    w_out = normal_values(seeds[10], (HID, FIELDS * LEVELS), HID ** -0.5, 0.25)
    target = normal_values(seeds[11], (LEVELS,), 1.0, 4.0, ((0, 8),), jnp.float32)
    coupling = normal_values(seeds[12], (NTOT, LEVELS, LEVELS), LEVELS ** -0.5, 1.0, (), jnp.float32)
    return dict(state=state, wave_table=wave_table, lat_table=lat_table, lat_weight=lat_weight, legendre=legendre, w_in=w_in, b_in=b_in, w_lat=w_lat, w_mid=w_mid, b_mid=b_mid, w_out=w_out, target=target, coupling=coupling)


time_step = 0.5
nudge_rate = 0.5
diffusion = 0.5


def tables(wave_table):
    longitude = jnp.arange(NLON, dtype=jnp.int32)
    phase_int = (wave_table[:, None] * longitude[None, :]) % NLON
    angles = phase_int.astype(jnp.float32) * (2.0 * math.pi / NLON)
    return jnp.cos(angles).astype(jnp.bfloat16), jnp.sin(angles).astype(jnp.bfloat16)


def reference(state, wave_table, lat_table, lat_weight, legendre, w_in, b_in, w_lat, w_mid, b_mid, w_out, target, coupling):
    degree = jnp.arange(NTOT, dtype=jnp.int32)
    live_mask = (degree[None, :] >= wave_table[:, None]).astype(jnp.float32)
    zero_slot = (wave_table == 0).astype(jnp.float32)
    cosine_table, sine_table = tables(wave_table)
    table32 = jnp.stack([cosine_table.astype(jnp.float32), -sine_table.astype(jnp.float32)], axis=1)
    legendre32 = legendre.astype(jnp.float32)
    lat_ids = jnp.arange(NLAT, dtype=jnp.float32)
    coslat = jnp.sin((lat_ids + 0.5) * (math.pi / NLAT))
    weight_total = jnp.sum(lat_weight)
    lat_scale = lat_weight * ((2.0 * MW) ** 0.5 / NLON)
    legconst = jnp.einsum('mtn,t->mn', legendre32, lat_weight)
    shrink = 1.0 / (1.0 + diffusion * (degree * (degree + 1)).astype(jnp.float32) / (NTOT * NTOT))

    def physics(inputs):
        vectors, lat_cos = inputs
        hidden = jnp.dot(w_in.T, vectors, preferred_element_type=jnp.float32) + b_in[:, None] + lat_cos * w_lat[:, None]
        hidden = jax.nn.silu(hidden).astype(jnp.bfloat16)
        hidden = jax.nn.silu(jnp.dot(w_mid.T, hidden, preferred_element_type=jnp.float32) + b_mid[:, None]).astype(jnp.bfloat16)
        return jnp.dot(w_out.T, hidden, preferred_element_type=jnp.float32).astype(jnp.bfloat16)

    def member(member_state):
        live5 = live_mask[:, None, None, None, :]
        state_bf = (member_state * live5).astype(jnp.bfloat16).astype(jnp.float32)
        fourier = jnp.einsum('mcfln,mtn->mcflt', state_bf, legendre32).astype(jnp.bfloat16)
        fourier32 = fourier.astype(jnp.float32)
        synthesis = jnp.einsum('mcflt,mcx->fltx', fourier32, table32)
        grid_bf = (synthesis * (MW ** -0.5)).astype(jnp.bfloat16)
        columns = grid_bf.reshape(FIELDS * LEVELS, NLAT, NLON).transpose(1, 0, 2)
        tendency = lax.map(physics, (columns, coslat))
        tend32 = tendency.transpose(1, 0, 2).reshape(FIELDS, LEVELS, NLAT, NLON).astype(jnp.float32)
        tendw = (jnp.einsum('fltx,mcx->mcflt', tend32, table32) * lat_scale).astype(jnp.bfloat16)
        tendw32 = tendw.astype(jnp.float32)
        mean_state = jnp.einsum('mlt,m,t->l', fourier32[:, 0, 0], zero_slot, lat_weight)
        mean_tend = jnp.einsum('mlt,m->l', tendw32[:, 0, 0], zero_slot)
        global_mean = (mean_state + time_step * mean_tend) / weight_total
        nudge_add = nudge_rate * (target - global_mean)
        spec_tend = jnp.einsum('mcflt,mtn->mcfln', tendw32, legendre32)
        extra_term = nudge_add[None, :, None] * (zero_slot[:, None] * legconst)[:, None, :]
        spec_tend = spec_tend.at[:, 0, 0].add(extra_term)
        explicit = (member_state + time_step * spec_tend) * live5
        new_temp = jnp.einsum('nlk,mckn->mcln', coupling, explicit[:, :, 0], precision=lax.Precision.HIGHEST)
        new_hum = explicit[:, :, 1] * shrink
        band_tend = tendency.transpose(1, 0, 2)[:, lat_table, :]
        return jnp.stack([new_temp, new_hum], axis=2), band_tend

    new_state, grid_tend = lax.map(member, jnp.moveaxis(state, 2, 0))
    return jnp.moveaxis(new_state, 0, 2), grid_tend
```

```python
import math

import jax
import jax.numpy as jnp
from jax import lax
from jax.experimental import pallas as pl
from jax.experimental.pallas import tpu as pltpu
from jax.sharding import PartitionSpec as P

F32 = jnp.float32
BF16 = jnp.bfloat16
WAVES = 32
LEVS = 8
MW = 256
NTOT = 256
NLAT = 384
NLON = 768
HID = 512
SLOTS = MW // WAVES
BAND = NLAT // WAVES
PAIRS = BAND // 2
LEVELS = 32
FEAT = 64
ROWL = LEVELS // LEVS
time_step = 0.5
nudge_rate = 0.5
diffusion = 0.5

VMEM = pl.BlockSpec(memory_space=pltpu.VMEM)
SMEM = pl.BlockSpec(memory_space=pltpu.SMEM)
HBM = pl.BlockSpec(memory_space=pltpu.HBM)


def call(body, outs, scratch, flops, operands, specs, name):
    operands = [
        pltpu.with_memory_space_constraint(o, pltpu.HBM) if spec in (HBM, SMEM) else o
        for o, spec in zip(operands, specs)
    ]
    return pl.pallas_call(
        body,
        out_shape=outs,
        in_specs=specs,
        out_specs=jax.tree.map(lambda o: HBM if isinstance(o, pl.MemoryRef) else VMEM, outs),
        scratch_shapes=scratch,
        compiler_params=pltpu.CompilerParams(vmem_limit_bytes=40 * 2**20),
        cost_estimate=pl.CostEstimate(flops=flops, bytes_accessed=2 * 10**6, transcendentals=0),
        name=name,
    )(*operands)


def out(shape, dtype):
    return jax.ShapeDtypeStruct(shape, dtype)


def live_row(waves_ref, first, j):
    lane = lax.broadcasted_iota(jnp.int32, (1, NTOT), 1)
    return (lane >= waves_ref[first + j]).astype(F32)


def pack_state(waves_ref, target_ref, state_hbm, send_ref, rows_ref, state_ref, sems):
    copies = [
        pltpu.make_async_copy(state_hbm.at[j], state_ref.at[j], sems.at[j]) for j in range(SLOTS)
    ]
    for copy in copies:
        copy.start()
    first = lax.axis_index("wave") * SLOTS
    lane = lax.broadcasted_iota(jnp.int32, (16, NTOT), 1)
    row = lax.broadcasted_iota(jnp.int32, (16, NTOT), 0)
    rider = jnp.zeros((16, NTOT), F32)
    for i in range(ROWL):
        rider = jnp.where((lane == 0) & (row == i), target_ref[i], rider)
    for j in range(SLOTS):
        live = live_row(waves_ref, first, j)
        extra = None
        if j < 2:
            extra = rider * jnp.full((16, NTOT), waves_ref[first + j] > 127, jnp.int32).astype(F32)
        copies[j].wait()
        for e in range(LEVS):
            for c in range(2):
                for f in range(2):
                    rows_ref[e, j, c * 8 + f * 4 : c * 8 + f * 4 + 4, :] = state_ref[j, c, e, f]
            block = rows_ref[e, j] * live
            send_ref[e, j] = (block if extra is None else block + extra).astype(BF16)


def sine_of(q):
    a = q * (2.0 * math.pi / NLON)
    b = a * a
    total = jnp.full_like(b, -2.5052108e-8)
    for factor in (2.7557319e-6, -1.9841270e-4, 8.3333333e-3, -1.6666667e-1, 1.0):
        total = total * b + factor
    return total * a


def prepare(
    lats_ref, weights_ref, lat_ref, weight_ref, waves_ref, legendre_ref, w_in_ref, b_in_ref, w_lat_ref, w_mid_ref,
    b_mid_ref, band_ref, const_ref, cos_t_hbm, sin_t_hbm, cos_hbm, sin_hbm, first_hbm, mid_hbm, bias_hbm, scale_hbm,
    hot_ref, cos_t_ref, sin_t_ref, cos_ref, sin_ref, first_ref, mid_ref, bias_ref, scale_ref, sems,
):
    pairs = (
        (cos_t_ref, cos_t_hbm),
        (sin_t_ref, sin_t_hbm),
        (cos_ref, cos_hbm),
        (sin_ref, sin_hbm),
        (first_ref, first_hbm),
        (mid_ref, mid_hbm),
        (bias_ref, bias_hbm),
        (scale_ref, scale_hbm),
    )
    copies = [pltpu.make_async_copy(a, b, sems.at[i]) for i, (a, b) in enumerate(pairs)]
    x = lax.broadcasted_iota(jnp.int32, (NLON, MW), 0)
    product = (x * waves_ref[...]).astype(F32)
    phase = product - NLON * jnp.floor(product * (1.0 / NLON) + 0.5)
    size = jnp.abs(phase)
    cosine = sine_of(NLON // 4 - size)
    sine = sine_of(jnp.where(size > NLON // 4, jnp.where(phase > 0, 1.0, -1.0) * (NLON // 2) - phase, phase))
    sine = -sine
    cos_t_ref[...] = (cosine * MW**-0.5).astype(BF16)
    copies[0].start()
    sin_t_ref[...] = (sine * MW**-0.5).astype(BF16)
    copies[1].start()
    cos_ref[...] = cosine.T.astype(BF16)
    copies[2].start()
    sin_ref[...] = sine.T.astype(BF16)
    copies[3].start()
    first_ref[...] = jnp.zeros_like(first_ref)
    half_in = (w_in_ref[...].astype(F32) * 0.5).astype(BF16)
    first_ref[0, :FEAT, :] = half_in
    first_ref[1, FEAT:, :] = half_in
    copies[4].start()
    mid_ref[...] = (w_mid_ref[...].astype(F32) * 0.5).astype(BF16)
    copies[5].start()
    lane = lax.broadcasted_iota(jnp.int32, (1, BAND * FEAT), 1)
    scale = jnp.zeros((1, BAND * FEAT), F32)
    own = lax.axis_index("wave") * BAND
    for b in range(BAND):
        t = lats_ref[own + b]
        here = (lane >= b * FEAT) & (lane < (b + 1) * FEAT)
        scale = jnp.where(here, weights_ref[t] * ((2.0 * MW) ** 0.5 / NLON), scale)
        at = jnp.full((1, HID), t, jnp.int32).astype(F32)
        coslat = jnp.sin((at + 0.5) * (math.pi / NLAT))
        bias_ref[b : b + 1, :] = 0.5 * (b_in_ref[...] + coslat * w_lat_ref[...])
    bias_ref[BAND : BAND + 1, :] = 0.5 * b_mid_ref[...]
    copies[6].start()
    scale_ref[...] = scale
    copies[7].start()

    t = lax.broadcasted_iota(jnp.int32, (NLAT, NLAT), 0)
    hot = (t == lat_ref[...]).astype(F32).T
    for i in range(NLAT // 128):
        hot_ref[i] = hot[:, i * 128 : (i + 1) * 128]
    pick = []
    for parity in range(2):
        parts = [
            jnp.concatenate(
                [hot_ref[i, pl.ds(2 * p + parity, WAVES, stride=BAND), :] for p in range(PAIRS)], axis=0
            )
            for i in range(NLAT // 128)
        ]
        pick.append(jnp.concatenate(parts, axis=1).astype(BF16))
    weight = weight_ref[...]
    high = weight.astype(BF16)
    low = (weight - high.astype(F32)).astype(BF16)
    row = lax.broadcasted_iota(jnp.int32, (16, NLAT), 0)
    both = jnp.where(row == 0, high.astype(F32), jnp.where(row == 1, low.astype(F32), 0.0))
    both = both.astype(BF16)
    for j in range(SLOTS):
        block = legendre_ref[j]
        for parity in range(2):
            band_ref[j, :, parity * NTOT : (parity + 1) * NTOT] = jnp.dot(
                pick[parity], block, preferred_element_type=F32
            ).astype(BF16)
        sums = jnp.dot(both, block, preferred_element_type=F32)
        const_ref[j : j + 1, :] = jnp.sum(sums, axis=0, keepdims=True)
    for copy in copies:
        copy.wait()


def to_fourier(
    waves_ref, recv_ref, band_ref, fourier_ref, state_ref, target_ref, rows_ref, both_ref, total_ref
):
    first = lax.axis_index("wave") * SLOTS
    both_ref[...] = jnp.zeros_like(both_ref)
    target = jnp.zeros((LEVELS, 1), F32)
    for j in range(SLOTS):
        live = live_row(waves_ref, first, j)
        k = j % 2
        for src in range(LEVS):
            block = recv_ref[src, j].astype(F32)
            for c in range(2):
                for f in range(2):
                    at = f * LEVELS + src * ROWL
                    rows_ref[k, c, at : at + 4, :] = block[c * 8 + f * 4 : c * 8 + f * 4 + 4, :]
        for c in range(2):
            if j < 2 and c == 0:
                here = jnp.full((LEVELS, 1), waves_ref[first + j] > 127, jnp.int32).astype(F32)
                target = target + here * rows_ref[k, 0, :LEVELS, :1]
            part = (rows_ref[k, c] * live).astype(BF16)
            state_ref[j, c] = part
            both_ref[k, c * 128 : c * 128 + 64, :NTOT] = part
            both_ref[k, c * 128 + 64 : c * 128 + 128, NTOT:] = part
        sums = lax.dot_general(
            band_ref[j], both_ref[k], (((1,), (1,)), ((), ())), preferred_element_type=F32
        )
        for c in range(2):
            for p in range(PAIRS):
                total_ref[c * PAIRS + p, pl.ds(j, WAVES, stride=SLOTS), :] = sums[
                    p * WAVES : (p + 1) * WAVES, c * 128 : (c + 1) * 128
                ]
    target_ref[...] = jnp.broadcast_to(target, (LEVELS, 128))
    for i in range(2 * PAIRS):
        fourier_ref[:, i * 128 : (i + 1) * 128] = total_ref[i].astype(BF16)


def half_silu(u):
    return (u + u * jnp.tanh(u)).astype(BF16)


TILE = 256


def dot_lanes(a, b):
    return lax.dot_general(a, b, (((1,), (1,)), ((), ())), preferred_element_type=F32)


def columns(
    coef_ref, cos_t_hbm, sin_t_hbm, first_hbm, bias_hbm, mid_hbm, last_hbm, cos_hbm, sin_hbm, scale_hbm,
    tendw_ref, grid_hbm, values_ref, grid_ref,
    cos_t_ref, sin_t_ref, first_ref, bias_ref, mid_ref, last_ref, cos_ref, sin_ref, scale_ref, sems, grid_sems,
):
    pairs = (
        (cos_t_hbm, cos_t_ref),
        (sin_t_hbm, sin_t_ref),
        (first_hbm, first_ref),
        (bias_hbm, bias_ref),
        (mid_hbm, mid_ref),
        (last_hbm, last_ref),
        (cos_hbm, cos_ref),
        (sin_hbm, sin_ref),
        (scale_hbm, scale_ref),
    )
    copies = [pltpu.make_async_copy(a, b, sems.at[i]) for i, (a, b) in enumerate(pairs)]
    for copy in copies:
        copy.start()

    def grid_copy(p):
        rows = pl.ds(2 * p, 2)
        return pltpu.make_async_copy(grid_ref.at[rows], grid_hbm.at[rows], grid_sems.at[p])

    half = BAND * FEAT
    copies[0].wait()
    copies[1].wait()
    values = jnp.dot(cos_t_ref[...], coef_ref[:, :half], preferred_element_type=F32)
    values += jnp.dot(sin_t_ref[...], coef_ref[:, half:], preferred_element_type=F32)
    for p in range(PAIRS):
        values_ref[p] = values[:, p * 128 : (p + 1) * 128].astype(BF16)
    for copy in copies[2:6]:
        copy.wait()

    def pair(p, carry):
        for tile in range(NLON // TILE):
            rows = slice(tile * TILE, (tile + 1) * TILE)
            v = values_ref[p, rows, :]
            hidden = [
                half_silu(
                    jnp.dot(v, first_ref[q], preferred_element_type=F32)
                    + bias_ref[pl.ds(2 * p + q, 1), :]
                )
                for q in range(2)
            ]
            hidden = [
                half_silu(
                    jnp.dot(h, mid_ref[...], preferred_element_type=F32)
                    + bias_ref[BAND : BAND + 1, :]
                )
                for h in hidden
            ]
            for q in range(2):
                grid_ref[2 * p + q, :, rows] = dot_lanes(last_ref[...], hidden[q]).astype(BF16)
        grid_copy(p).start()
        return carry

    lax.fori_loop(0, PAIRS, pair, 0)
    for copy in copies[6:]:
        copy.wait()
    tend = grid_ref[...].reshape(half, NLON)
    scale = scale_ref[...]
    for c, table in enumerate((cos_ref, sin_ref)):
        tendw_ref[:, c * half : (c + 1) * half] = (dot_lanes(table[...], tend) * scale).astype(BF16)
    for p in range(PAIRS):
        grid_copy(p).wait()


def to_spectral(
    waves_ref, recv_ref, band_ref, state_ref, const_ref, weight_ref, target_ref, coupling_ref,
    send_ref, wide_ref, temp_ref, rows_ref, matrix_ref,
):
    first = lax.axis_index("wave") * SLOTS
    for i in range(2 * PAIRS):
        wide_ref[i] = recv_ref[:, i * 128 : (i + 1) * 128].astype(F32)
    for i in range(2):
        matrix_ref[i] = coupling_ref[:, i * 128 : (i + 1) * 128]
    target = target_ref[:, :1]
    weight_total = jnp.sum(weight_ref[...], axis=1, keepdims=True)
    degree = lax.broadcasted_iota(jnp.int32, (1, NTOT), 1)
    shrink = 1.0 / (1.0 + diffusion * (degree * (degree + 1)).astype(F32) / (NTOT * NTOT))
    for j in range(SLOTS):
        live = live_row(waves_ref, first, j)
        is_zero = (jnp.full((1, NTOT), waves_ref[first + j], jnp.int32) == 0).astype(F32)
        block = jnp.concatenate(
            [
                jnp.concatenate(
                    [wide_ref[c * PAIRS + p, pl.ds(j, WAVES, stride=SLOTS), :] for c in range(2)],
                    axis=1,
                )
                for p in range(PAIRS)
            ],
            axis=0,
        )
        turned = block.T
        tend_sum = jnp.sum(turned[:128], axis=1, keepdims=True)
        parts = turned.astype(BF16)
        even = jnp.concatenate([parts[:64], parts[128:192]], axis=0)
        odd = jnp.concatenate([parts[64:128], parts[192:]], axis=0)
        spec = jnp.dot(even, band_ref[j, :, :NTOT], preferred_element_type=F32)
        spec += jnp.dot(odd, band_ref[j, :, NTOT:], preferred_element_type=F32)
        const = const_ref[j : j + 1, :]
        for c in range(2):
            old = state_ref[j, c].astype(F32)
            old_temp, old_hum = old[:LEVELS], old[LEVELS:]
            temp = spec[c * 64 : c * 64 + 32]
            hum = spec[c * 64 + 32 : c * 64 + 64]
            if c == 0:
                mean = jnp.sum(old_temp * const, axis=1, keepdims=True)
                mean += time_step * (tend_sum[:32] + tend_sum[64:96])
                nudge = nudge_rate * (target - mean / weight_total)
                temp = temp + nudge * (const * is_zero)
            temp_ref[j * 2 + c] = (old_temp + time_step * temp) * live
            hum = (old_hum + time_step * hum) * (live * shrink)
            for d in range(LEVS):
                rows_ref[d, j, c * 8 + 4 : c * 8 + 8, :] = hum[d * 4 : d * 4 + 4]
    group = 4
    for g in range(2 * SLOTS // group):

        def step(k, totals):
            matrix = jnp.concatenate(
                [matrix_ref[i, pl.ds(k, LEVELS, stride=LEVELS), :] for i in range(2)], axis=1
            )
            return tuple(
                totals[q] + matrix * temp_ref[g * group + q, pl.ds(k, 1), :] for q in range(group)
            )

        zero = jnp.zeros((LEVELS, NTOT), F32)
        totals = lax.fori_loop(0, LEVELS, step, (zero,) * group, unroll=4)
        for q in range(group):
            j, c = divmod(g * group + q, 2)
            for d in range(LEVS):
                rows_ref[d, j, c * 8 : c * 8 + 4, :] = totals[q][d * 4 : d * 4 + 4]
    send_ref[...] = rows_ref[...].astype(BF16)


def unpack_state(recv_ref, state_ref):
    for e in range(LEVS):
        for j in range(SLOTS):
            block = recv_ref[e, j].astype(F32)
            for c in range(2):
                for f in range(2):
                    state_ref[j, c, e, f] = block[c * 8 + f * 4 : c * 8 + f * 4 + 4, :]


def per_device(
    state,
    wave_table,
    lat_table,
    lat_weight,
    legendre,
    w_in,
    b_in,
    w_lat,
    w_mid,
    b_mid,
    w_out,
    target,
    coupling,
):
    message = (LEVS, SLOTS, 16, NTOT)
    sent = call(
        pack_state,
        out(message, BF16),
        [
            pltpu.VMEM(message, F32),
            pltpu.VMEM(state.shape, F32),
            pltpu.SemaphoreType.DMA((SLOTS,)),
        ],
        10**8,
        (wave_table, target, state),
        [SMEM] * 2 + [HBM],
        "pack_state",
    )
    members = lax.all_to_all(sent, "lev", 0, 0, tiled=True)
    table, turned, weights = (NLON, MW), (MW, NLON), (2, 2 * FEAT, HID)
    made = [
        (table, BF16),
        (table, BF16),
        (turned, BF16),
        (turned, BF16),
        (weights, BF16),
        ((HID, HID), BF16),
        ((16, HID), F32),
        ((1, BAND * FEAT), F32),
    ]
    band, const, cos_t, sin_t, cos, sin, first, mid, bias, scale = call(
        prepare,
        (
            out((SLOTS, PAIRS * WAVES, 2 * NTOT), BF16),
            out((SLOTS, NTOT), F32),
            *(pltpu.HBM(*m) for m in made),
        ),
        [
            pltpu.VMEM((NLAT // 128, NLAT, 128), F32),
            *(pltpu.VMEM(*m) for m in made),
            pltpu.SemaphoreType.DMA((len(made),)),
        ],
        6 * 10**9,
        (
            lat_table,
            lat_weight,
            lat_table[None],
            lat_weight[None],
            wave_table[None],
            legendre,
            w_in,
            b_in[None],
            w_lat[None],
            w_mid,
            b_mid[None],
        ),
        [SMEM] * 2 + [VMEM] * 9,
        "prepare",
    )
    fourier, state_bf, target_all = call(
        to_fourier,
        (
            out((MW, 2 * BAND * FEAT), BF16),
            out((SLOTS, 2, FEAT, NTOT), BF16),
            out((LEVELS, 128), F32),
        ),
        [
            pltpu.VMEM((2, 2, FEAT, NTOT), F32),
            pltpu.VMEM((2, NTOT, 2 * NTOT), BF16),
            pltpu.VMEM((2 * PAIRS, MW, 128), F32),
        ],
        10**9,
        (wave_table, members, band),
        [SMEM] + [VMEM] * 2,
        "to_fourier",
    )
    coef = lax.all_to_all(fourier, "wave", 0, 0, tiled=True)
    tendw, grid = call(
        columns,
        (
            out((MW, 2 * BAND * FEAT), BF16),
            pltpu.HBM((BAND, FEAT, NLON), BF16),
        ),
        [
            pltpu.VMEM((PAIRS, NLON, 128), BF16),
            pltpu.VMEM((BAND, FEAT, NLON), BF16),
            *(pltpu.VMEM(v.shape, v.dtype) for v in (cos_t, sin_t, first, bias, mid, w_out.T, cos, sin, scale)),
            pltpu.SemaphoreType.DMA((9,)),
            pltpu.SemaphoreType.DMA((PAIRS,)),
        ],
        10**10,
        (coef, cos_t, sin_t, first, bias, mid, w_out.T, cos, sin, scale),
        [VMEM] + [HBM] * 9,
        "columns",
    )
    back = lax.all_to_all(tendw, "wave", 0, 0, tiled=True)
    moved = call(
        to_spectral,
        out(message, BF16),
        [
            pltpu.VMEM((2 * PAIRS, MW, 128), F32),
            pltpu.VMEM((2 * SLOTS, LEVELS, NTOT), F32),
            pltpu.VMEM(message, F32),
            pltpu.VMEM((2, LEVELS * LEVELS, 128), F32),
        ],
        10**9,
        (
            wave_table,
            back,
            band,
            state_bf,
            const,
            lat_weight[None],
            target_all,
            jnp.transpose(coupling, (1, 2, 0)).reshape(LEVELS * LEVELS, NTOT),
        ),
        [SMEM] + [VMEM] * 7,
        "to_spectral",
    )
    returned = lax.all_to_all(moved, "lev", 0, 0, tiled=True)
    new_state = call(
        unpack_state,
        out(state.shape, F32),
        [],
        10**8,
        (returned,),
        [VMEM],
        "unpack_state",
    )
    return new_state, jnp.transpose(grid, (1, 0, 2))[None]


def solution(mesh):
    placed = (
        P("wave", None, None, None, "lev", None),
        P(),
        P(),
        P(),
        P("wave", None, None),
        P(),
        P(),
        P(),
        P(),
        P(),
        P(),
        P("lev"),
        P(),
    )
    return jax.shard_map(
        per_device,
        mesh=mesh,
        in_specs=placed,
        out_specs=(P("wave", None, None, None, "lev", None), P("lev", None, "wave", None)),
        check_vma=False,
    )
```

```python
import math

import jax
import jax.numpy as jnp
from jax import lax
from jax.experimental import pallas as pl
from jax.experimental.pallas import tpu as pltpu
from jax.sharding import PartitionSpec as P

F32 = jnp.float32
BF16 = jnp.bfloat16
WAVES = 32
LEVS = 8
MW = 256
NTOT = 256
NLAT = 384
NLON = 768
HID = 512
SLOTS = MW // WAVES
BAND = NLAT // WAVES
PAIRS = BAND // 2
LEVELS = 32
FEAT = 64
ROWL = LEVELS // LEVS
time_step = 0.5
nudge_rate = 0.5
diffusion = 0.5

VMEM = pl.BlockSpec(memory_space=pltpu.VMEM)
SMEM = pl.BlockSpec(memory_space=pltpu.SMEM)
HBM = pl.BlockSpec(memory_space=pltpu.HBM)


def call(body, outs, scratch, flops, operands, specs, name):
    operands = [
        pltpu.with_memory_space_constraint(o, pltpu.HBM) if spec in (HBM, SMEM) else o
        for o, spec in zip(operands, specs)
    ]
    return pl.pallas_call(
        body,
        out_shape=outs,
        in_specs=specs,
        out_specs=jax.tree.map(lambda o: HBM if isinstance(o, pl.MemoryRef) else VMEM, outs),
        scratch_shapes=scratch,
        compiler_params=pltpu.CompilerParams(vmem_limit_bytes=40 * 2**20),
        cost_estimate=pl.CostEstimate(flops=flops, bytes_accessed=2 * 10**6, transcendentals=0),
        name=name,
    )(*operands)


def out(shape, dtype):
    return jax.ShapeDtypeStruct(shape, dtype)


def live_row(waves_ref, first, j):
    lane = lax.broadcasted_iota(jnp.int32, (1, NTOT), 1)
    return (lane >= waves_ref[first + j]).astype(F32)


def fold(first, second, q, m, extra):
    lane = lax.broadcasted_iota(jnp.int32, first.shape, 1)
    turned = pltpu.roll(second, m, axis=1)
    block = lax.broadcasted_iota(jnp.int32, extra.shape, 1)
    extra = jnp.where(block == q, pltpu.roll(turned[:, 128:], q + 1, axis=1), extra)
    return jnp.where(lane >= m, first, turned), extra


def unfold(both, extra, q, m):
    lane = lax.broadcasted_iota(jnp.int32, both.shape, 1)
    block = lax.broadcasted_iota(jnp.int32, extra.shape, 1)
    last = jnp.where(block == 127, pltpu.roll(extra, 127 - q, axis=1), both[:, 128:])
    turned = jnp.concatenate([both[:, :128], last], axis=1)
    turned = pltpu.roll(turned, (NTOT - m) & (NTOT - 1), axis=1)
    return jnp.where(lane >= m, both, 0.0), jnp.where(lane >= NTOT - 1 - m, turned, 0.0)


def pack_state(
    waves_hbm, target_hbm, state_hbm, send_ref, rows_ref, state_ref, waves_ref, target_ref, sems, small_sems
):
    copies = [
        pltpu.make_async_copy(state_hbm.at[j], state_ref.at[j], sems.at[j]) for j in range(SLOTS)
    ]
    waves_copy = pltpu.make_async_copy(waves_hbm, waves_ref, small_sems.at[0])
    target_copy = pltpu.make_async_copy(target_hbm, target_ref, small_sems.at[1])
    for copy in (*copies, waves_copy, target_copy):
        copy.start()
    target_copy.wait()
    waves_copy.wait()
    first = lax.axis_index("wave") * SLOTS
    lane = lax.broadcasted_iota(jnp.int32, (16, 128), 1)
    row = lax.broadcasted_iota(jnp.int32, (16, 128), 0)
    rider = jnp.zeros((16, 128), F32)
    for i in range(ROWL):
        rider = jnp.where((lane == SLOTS // 2) & (row == i), target_ref[i], rider)
    extra = jnp.concatenate([rider] * LEVS, axis=0)
    for q in range(SLOTS // 2):
        for j in (2 * q, 2 * q + 1):
            copies[j].wait()
            for e in range(LEVS):
                for c in range(2):
                    for f in range(2):
                        at = c * 8 + f * 4
                        rows_ref[j, e, at : at + 4, :] = state_ref[j, c, e, f]
        flat = [rows_ref[j].reshape(LEVS * 16, NTOT) for j in (2 * q, 2 * q + 1)]
        both, extra = fold(*flat, q, waves_ref[first + 2 * q], extra)
        send_ref[:, :, q * NTOT : (q + 1) * NTOT] = both.astype(BF16).reshape(LEVS, 16, NTOT)
    send_ref[:, :, 4 * NTOT :] = extra.astype(BF16).reshape(LEVS, 16, 128)


def sine_of(q):
    a = q * (2.0 * math.pi / NLON)
    b = a * a
    total = jnp.full_like(b, -2.5052108e-8)
    for factor in (2.7557319e-6, -1.9841270e-4, 8.3333333e-3, -1.6666667e-1, 1.0):
        total = total * b + factor
    return total * a


def prepare(
    lats_ref, weights_ref, lat_ref, weight_ref, waves_ref, legendre_hbm, w_in_ref, b_in_ref, w_lat_ref, w_mid_ref,
    b_mid_ref, band_ref, const_ref, cos_t_hbm, sin_t_hbm, cos_hbm, sin_hbm, first_hbm, mid_hbm, bias_hbm, scale_hbm,
    hot_ref, cos_t_ref, sin_t_ref, cos_ref, sin_ref, first_ref, mid_ref, bias_ref, scale_ref, legendre_ref, sems, in_sem,
):
    pairs = (
        (cos_t_ref, cos_t_hbm),
        (sin_t_ref, sin_t_hbm),
        (cos_ref, cos_hbm),
        (sin_ref, sin_hbm),
        (first_ref, first_hbm),
        (mid_ref, mid_hbm),
        (bias_ref, bias_hbm),
        (scale_ref, scale_hbm),
    )
    copies = [pltpu.make_async_copy(a, b, sems.at[i]) for i, (a, b) in enumerate(pairs)]
    legendre_copy = pltpu.make_async_copy(legendre_hbm, legendre_ref, in_sem)
    legendre_copy.start()
    x = lax.broadcasted_iota(jnp.int32, (NLON, MW), 0)
    product = (x * waves_ref[...]).astype(F32)
    phase = product - NLON * jnp.floor(product * (1.0 / NLON) + 0.5)
    size = jnp.abs(phase)
    cosine = sine_of(NLON // 4 - size)
    sine = sine_of(jnp.where(size > NLON // 4, jnp.where(phase > 0, 1.0, -1.0) * (NLON // 2) - phase, phase))
    sine = -sine
    cos_t_ref[...] = (cosine * MW**-0.5).astype(BF16)
    copies[0].start()
    sin_t_ref[...] = (sine * MW**-0.5).astype(BF16)
    copies[1].start()
    cos_ref[...] = cosine.T.astype(BF16)
    copies[2].start()
    sin_ref[...] = sine.T.astype(BF16)
    copies[3].start()
    first_ref[...] = jnp.zeros_like(first_ref)
    half_in = (w_in_ref[...].astype(F32) * 0.5).astype(BF16)
    first_ref[0, :FEAT, :] = half_in
    first_ref[1, FEAT:, :] = half_in
    copies[4].start()
    mid_ref[...] = (w_mid_ref[...].astype(F32) * 0.5).astype(BF16)
    copies[5].start()
    lane = lax.broadcasted_iota(jnp.int32, (1, BAND * FEAT), 1)
    scale = jnp.zeros((1, BAND * FEAT), F32)
    own = lax.axis_index("wave") * BAND
    for b in range(BAND):
        t = lats_ref[own + b]
        here = (lane >= b * FEAT) & (lane < (b + 1) * FEAT)
        scale = jnp.where(here, weights_ref[t] * ((2.0 * MW) ** 0.5 / NLON), scale)
        at = jnp.full((1, HID), t, jnp.int32).astype(F32)
        coslat = jnp.sin((at + 0.5) * (math.pi / NLAT))
        bias_ref[b : b + 1, :] = 0.5 * (b_in_ref[...] + coslat * w_lat_ref[...])
    bias_ref[BAND : BAND + 1, :] = 0.5 * b_mid_ref[...]
    copies[6].start()
    scale_ref[...] = scale
    copies[7].start()

    t = lax.broadcasted_iota(jnp.int32, (NLAT, NLAT), 0)
    hot = (t == lat_ref[...]).astype(F32).T
    for i in range(NLAT // 128):
        hot_ref[i] = hot[:, i * 128 : (i + 1) * 128]
    pick = []
    for parity in range(2):
        parts = [
            jnp.concatenate(
                [hot_ref[i, pl.ds(2 * p + parity, WAVES, stride=BAND), :] for p in range(PAIRS)], axis=0
            )
            for i in range(NLAT // 128)
        ]
        pick.append(jnp.concatenate(parts, axis=1).astype(BF16))
    weight = weight_ref[...]
    high = weight.astype(BF16)
    low = (weight - high.astype(F32)).astype(BF16)
    row = lax.broadcasted_iota(jnp.int32, (16, NLAT), 0)
    both = jnp.where(row == 0, high.astype(F32), jnp.where(row == 1, low.astype(F32), 0.0))
    both = both.astype(BF16)
    legendre_copy.wait()
    for j in range(SLOTS):
        block = legendre_ref[j]
        for parity in range(2):
            band_ref[j, :, parity * NTOT : (parity + 1) * NTOT] = jnp.dot(
                pick[parity], block, preferred_element_type=F32
            ).astype(BF16)
        sums = jnp.dot(both, block, preferred_element_type=F32)
        const_ref[j : j + 1, :] = jnp.sum(sums, axis=0, keepdims=True)
    for copy in copies:
        copy.wait()


def to_fourier(
    waves_ref, recv_ref, band_ref, fourier_ref, state_ref, target_ref, rows_ref, both_ref, total_ref
):
    first = lax.axis_index("wave") * SLOTS
    both_ref[...] = jnp.zeros_like(both_ref)
    extra = recv_ref[:, :, 4 * NTOT :].astype(F32)
    for src in range(LEVS):
        at = src * ROWL
        target_ref[at : at + ROWL, :] = jnp.broadcast_to(
            extra[src, :ROWL, SLOTS // 2 : SLOTS // 2 + 1], (ROWL, 128)
        )
    extra = extra.reshape(LEVS * 16, 128)
    for j in range(SLOTS):
        k = j % 2
        q = j // 2
        if k == 0:
            both = recv_ref[:, :, q * NTOT : (q + 1) * NTOT].astype(F32).reshape(LEVS * 16, NTOT)
            split = unfold(both, extra, q, waves_ref[first + j])
        for src in range(LEVS):
            block = split[k][src * 16 : (src + 1) * 16]
            for c in range(2):
                for f in range(2):
                    at = f * LEVELS + src * ROWL
                    rows_ref[k, c, at : at + 4, :] = block[c * 8 + f * 4 : c * 8 + f * 4 + 4, :]
        for c in range(2):
            part = rows_ref[k, c].astype(BF16)
            state_ref[j, c] = part
            both_ref[k, c * 128 : c * 128 + 64, :NTOT] = part
            both_ref[k, c * 128 + 64 : c * 128 + 128, NTOT:] = part
        sums = lax.dot_general(
            band_ref[j], both_ref[k], (((1,), (1,)), ((), ())), preferred_element_type=F32
        )
        for c in range(2):
            for p in range(PAIRS):
                total_ref[c * PAIRS + p, pl.ds(j, WAVES, stride=SLOTS), :] = sums[
                    p * WAVES : (p + 1) * WAVES, c * 128 : (c + 1) * 128
                ]
    for i in range(2 * PAIRS):
        fourier_ref[:, i * 128 : (i + 1) * 128] = total_ref[i].astype(BF16)


def half_silu(u):
    return (u + u * jnp.tanh(u)).astype(BF16)


def dot_lanes(a, b):
    return lax.dot_general(a, b, (((1,), (1,)), ((), ())), preferred_element_type=F32)


def columns(
    coef_ref, cos_t_hbm, sin_t_hbm, first_hbm, bias_hbm, mid_hbm, last_hbm, cos_hbm, sin_hbm, scale_hbm,
    tendw_ref, grid_hbm, values_ref, grid_ref, hidden_ref,
    cos_t_ref, sin_t_ref, first_ref, bias_ref, mid_ref, last_ref, cos_ref, sin_ref, scale_ref, sems, grid_sems,
):
    pairs = (
        (cos_t_hbm, cos_t_ref),
        (sin_t_hbm, sin_t_ref),
        (first_hbm, first_ref),
        (bias_hbm, bias_ref),
        (mid_hbm, mid_ref),
        (last_hbm, last_ref),
        (cos_hbm, cos_ref),
        (sin_hbm, sin_ref),
        (scale_hbm, scale_ref),
    )
    copies = [pltpu.make_async_copy(a, b, sems.at[i]) for i, (a, b) in enumerate(pairs)]
    for copy in copies:
        copy.start()

    def grid_copy(p):
        rows = pl.ds(2 * p, 2)
        return pltpu.make_async_copy(grid_ref.at[rows], grid_hbm.at[rows], grid_sems.at[p])

    half = BAND * FEAT
    copies[0].wait()
    copies[1].wait()
    values = jnp.dot(cos_t_ref[...], coef_ref[:, :half], preferred_element_type=F32)
    values += jnp.dot(sin_t_ref[...], coef_ref[:, half:], preferred_element_type=F32)
    for p in range(PAIRS):
        values_ref[p] = values[:, p * 128 : (p + 1) * 128].astype(BF16)
    for copy in copies[2:6]:
        copy.wait()

    for p in range(PAIRS):
        for q in range(2):
            hidden = jnp.dot(values_ref[p], first_ref[q], preferred_element_type=F32)
            hidden_ref[q, 0] = half_silu(hidden + bias_ref[2 * p + q : 2 * p + q + 1, :])
            hidden = jnp.dot(hidden_ref[q, 0], mid_ref[...], preferred_element_type=F32)
            hidden_ref[q, 1] = half_silu(hidden + bias_ref[BAND : BAND + 1, :])
            grid_ref[2 * p + q] = dot_lanes(last_ref[...], hidden_ref[q, 1]).astype(BF16)
        grid_copy(p).start()
    for copy in copies[6:]:
        copy.wait()
    tend = grid_ref[...].reshape(half, NLON)
    scale = scale_ref[...]
    for c, table in enumerate((cos_ref, sin_ref)):
        tendw_ref[:, c * half : (c + 1) * half] = (dot_lanes(table[...], tend) * scale).astype(BF16)
    for p in range(PAIRS):
        grid_copy(p).wait()


def to_spectral(
    waves_ref, recv_ref, band_ref, state_ref, const_ref, weight_ref, target_ref, coupling_ref,
    send_ref, wide_ref, temp_ref, rows_ref,
):
    first = lax.axis_index("wave") * SLOTS
    for i in range(2 * PAIRS):
        wide_ref[i] = recv_ref[:, i * 128 : (i + 1) * 128].astype(F32)
    target = target_ref[:, :1]
    weight_total = jnp.sum(weight_ref[...], axis=1, keepdims=True)
    degree = lax.broadcasted_iota(jnp.int32, (1, NTOT), 1)
    shrink = 1.0 / (1.0 + diffusion * (degree * (degree + 1)).astype(F32) / (NTOT * NTOT))
    for j in range(SLOTS):
        live = live_row(waves_ref, first, j)
        is_zero = (jnp.full((1, NTOT), waves_ref[first + j], jnp.int32) == 0).astype(F32)
        block = jnp.concatenate(
            [
                jnp.concatenate(
                    [wide_ref[c * PAIRS + p, pl.ds(j, WAVES, stride=SLOTS), :] for c in range(2)],
                    axis=1,
                )
                for p in range(PAIRS)
            ],
            axis=0,
        )
        turned = block.T
        tend_sum = jnp.sum(turned[:128], axis=1, keepdims=True)
        parts = turned.astype(BF16)
        even = jnp.concatenate([parts[:64], parts[128:192]], axis=0)
        odd = jnp.concatenate([parts[64:128], parts[192:]], axis=0)
        spec = jnp.dot(even, band_ref[j, :, :NTOT], preferred_element_type=F32)
        spec += jnp.dot(odd, band_ref[j, :, NTOT:], preferred_element_type=F32)
        const = const_ref[j : j + 1, :]
        for c in range(2):
            old = state_ref[j, c].astype(F32)
            old_temp, old_hum = old[:LEVELS], old[LEVELS:]
            temp = spec[c * 64 : c * 64 + 32]
            hum = spec[c * 64 + 32 : c * 64 + 64]
            if c == 0:
                mean = jnp.sum(old_temp * const, axis=1, keepdims=True)
                mean += time_step * (tend_sum[:32] + tend_sum[64:96])
                nudge = nudge_rate * (target - mean / weight_total)
                temp = temp + nudge * (const * is_zero)
            temp_ref[j * 2 + c] = (old_temp + time_step * temp) * live
            hum = (old_hum + time_step * hum) * (live * shrink)
            for d in range(LEVS):
                rows_ref[j, d, c * 8 + 4 : c * 8 + 8, :] = hum[d * 4 : d * 4 + 4]
    group = 4
    for g in range(2 * SLOTS // group):
        for half in range(2):
            lanes = slice(half * 128, (half + 1) * 128)
            temps = [temp_ref[g * group + i, :, lanes] for i in range(group)]
            for level in range(LEVELS):
                matrix = coupling_ref[level * LEVELS : (level + 1) * LEVELS, lanes]
                for i in range(group):
                    j, c = divmod(g * group + i, 2)
                    at = c * 8 + level % ROWL
                    rows_ref[j, level // ROWL, at : at + 1, lanes] = jnp.sum(
                        matrix * temps[i], axis=0, keepdims=True
                    )
    extra = jnp.zeros((LEVS * 16, 128), F32)
    for q in range(SLOTS // 2):
        flat = [rows_ref[j].reshape(LEVS * 16, NTOT) for j in (2 * q, 2 * q + 1)]
        both, extra = fold(*flat, q, waves_ref[first + 2 * q], extra)
        send_ref[:, :, q * NTOT : (q + 1) * NTOT] = both.astype(BF16).reshape(LEVS, 16, NTOT)
    send_ref[:, :, 4 * NTOT :] = extra.astype(BF16).reshape(LEVS, 16, 128)


def unpack_state(waves_ref, recv_ref, state_hbm, state_ref, sems):
    copies = [
        pltpu.make_async_copy(state_ref.at[j], state_hbm.at[j], sems.at[j]) for j in range(SLOTS)
    ]
    first = lax.axis_index("wave") * SLOTS
    extra = recv_ref[:, :, 4 * NTOT :].astype(F32).reshape(LEVS * 16, 128)
    for q in range(SLOTS // 2):
        both = recv_ref[:, :, q * NTOT : (q + 1) * NTOT].astype(F32).reshape(LEVS * 16, NTOT)
        split = unfold(both, extra, q, waves_ref[first + 2 * q])
        for k in range(2):
            for e in range(LEVS):
                for c in range(2):
                    for f in range(2):
                        at = e * 16 + c * 8 + f * 4
                        state_ref[2 * q + k, c, e, f] = split[k][at : at + 4, :]
            copies[2 * q + k].start()
    for copy in copies:
        copy.wait()


def per_device(
    state,
    wave_table,
    lat_table,
    lat_weight,
    legendre,
    w_in,
    b_in,
    w_lat,
    w_mid,
    b_mid,
    w_out,
    target,
    coupling,
):
    message = (LEVS, 16, SLOTS // 2 * NTOT + 128)
    rows = (SLOTS, LEVS, 16, NTOT)
    sent = call(
        pack_state,
        out(message, BF16),
        [
            pltpu.VMEM(rows, F32),
            pltpu.VMEM(state.shape, F32),
            pltpu.SMEM((MW,), jnp.int32),
            pltpu.SMEM((ROWL,), F32),
            pltpu.SemaphoreType.DMA((SLOTS,)),
            pltpu.SemaphoreType.DMA((2,)),
        ],
        10**8,
        (wave_table, target, state),
        [HBM] * 3,
        "pack_state",
    )
    members = lax.all_to_all(sent, "lev", 0, 0, tiled=True)
    table, turned, weights = (NLON, MW), (MW, NLON), (2, 2 * FEAT, HID)
    made = [
        (table, BF16),
        (table, BF16),
        (turned, BF16),
        (turned, BF16),
        (weights, BF16),
        ((HID, HID), BF16),
        ((16, HID), F32),
        ((1, BAND * FEAT), F32),
    ]
    band, const, cos_t, sin_t, cos, sin, first, mid, bias, scale = call(
        prepare,
        (
            out((SLOTS, PAIRS * WAVES, 2 * NTOT), BF16),
            out((SLOTS, NTOT), F32),
            *(pltpu.HBM(*m) for m in made),
        ),
        [
            pltpu.VMEM((NLAT // 128, NLAT, 128), F32),
            *(pltpu.VMEM(*m) for m in made),
            pltpu.VMEM(legendre.shape, BF16),
            pltpu.SemaphoreType.DMA((len(made),)),
            pltpu.SemaphoreType.DMA,
        ],
        6 * 10**9,
        (
            lat_table,
            lat_weight,
            lat_table[None],
            lat_weight[None],
            wave_table[None],
            legendre,
            w_in,
            b_in[None],
            w_lat[None],
            w_mid,
            b_mid[None],
        ),
        [SMEM] * 2 + [VMEM] * 3 + [HBM] + [VMEM] * 5,
        "prepare",
    )
    fourier, state_bf, target_all = call(
        to_fourier,
        (
            out((MW, 2 * BAND * FEAT), BF16),
            out((SLOTS, 2, FEAT, NTOT), BF16),
            out((LEVELS, 128), F32),
        ),
        [
            pltpu.VMEM((2, 2, FEAT, NTOT), F32),
            pltpu.VMEM((2, NTOT, 2 * NTOT), BF16),
            pltpu.VMEM((2 * PAIRS, MW, 128), F32),
        ],
        10**9,
        (wave_table, members, band),
        [SMEM] + [VMEM] * 2,
        "to_fourier",
    )
    coef = lax.all_to_all(fourier, "wave", 0, 0, tiled=True)
    tendw, grid = call(
        columns,
        (
            out((MW, 2 * BAND * FEAT), BF16),
            pltpu.HBM((BAND, FEAT, NLON), BF16),
        ),
        [
            pltpu.VMEM((PAIRS, NLON, 128), BF16),
            pltpu.VMEM((BAND, FEAT, NLON), BF16),
            pltpu.VMEM((2, 2, NLON, HID), BF16),
            *(pltpu.VMEM(v.shape, v.dtype) for v in (cos_t, sin_t, first, bias, mid, w_out.T, cos, sin, scale)),
            pltpu.SemaphoreType.DMA((9,)),
            pltpu.SemaphoreType.DMA((PAIRS,)),
        ],
        10**10,
        (coef, cos_t, sin_t, first, bias, mid, w_out.T, cos, sin, scale),
        [VMEM] + [HBM] * 9,
        "columns",
    )
    back = lax.all_to_all(tendw, "wave", 0, 0, tiled=True)
    moved = call(
        to_spectral,
        out(message, BF16),
        [
            pltpu.VMEM((2 * PAIRS, MW, 128), F32),
            pltpu.VMEM((2 * SLOTS, LEVELS, NTOT), F32),
            pltpu.VMEM(rows, F32),
        ],
        10**9,
        (
            wave_table,
            back,
            band,
            state_bf,
            const,
            lat_weight[None],
            target_all,
            jnp.transpose(coupling, (1, 2, 0)).reshape(LEVELS * LEVELS, NTOT),
        ),
        [SMEM] + [VMEM] * 7,
        "to_spectral",
    )
    returned = lax.all_to_all(moved, "lev", 0, 0, tiled=True)
    new_state = call(
        unpack_state,
        pltpu.HBM(state.shape, F32),
        [pltpu.VMEM(state.shape, F32), pltpu.SemaphoreType.DMA((SLOTS,))],
        10**8,
        (wave_table, returned),
        [SMEM, VMEM],
        "unpack_state",
    )
    return new_state, jnp.transpose(grid, (1, 0, 2))[None]


def solution(mesh):
    placed = (
        P("wave", None, None, None, "lev", None),
        P(),
        P(),
        P(),
        P("wave", None, None),
        P(),
        P(),
        P(),
        P(),
        P(),
        P(),
        P("lev"),
        P(),
    )
    return jax.shard_map(
        per_device,
        mesh=mesh,
        in_specs=placed,
        out_specs=(P("wave", None, None, None, "lev", None), P("lev", None, "wave", None)),
        check_vma=False,
    )
```

```python
import math

import jax
import jax.numpy as jnp
from jax import lax
from jax.experimental import pallas as pl
from jax.experimental.pallas import tpu as pltpu
from jax.sharding import PartitionSpec as P

F32 = jnp.float32
BF16 = jnp.bfloat16
WAVES = 32
LEVS = 8
MW = 256
NTOT = 256
NLAT = 384
NLON = 768
HID = 512
SLOTS = MW // WAVES
BAND = NLAT // WAVES
PAIRS = BAND // 2
LEVELS = 32
FEAT = 64
ROWL = LEVELS // LEVS
time_step = 0.5
nudge_rate = 0.5
diffusion = 0.5

VMEM = pl.BlockSpec(memory_space=pltpu.VMEM)
SMEM = pl.BlockSpec(memory_space=pltpu.SMEM)
HBM = pl.BlockSpec(memory_space=pltpu.HBM)


def call(body, outs, scratch, flops, operands, specs, name):
    operands = [
        pltpu.with_memory_space_constraint(o, pltpu.HBM) if spec in (HBM, SMEM) else o
        for o, spec in zip(operands, specs)
    ]
    return pl.pallas_call(
        body,
        out_shape=outs,
        in_specs=specs,
        out_specs=jax.tree.map(lambda o: HBM if isinstance(o, pl.MemoryRef) else VMEM, outs),
        scratch_shapes=scratch,
        compiler_params=pltpu.CompilerParams(vmem_limit_bytes=40 * 2**20),
        cost_estimate=pl.CostEstimate(flops=flops, bytes_accessed=2 * 10**6, transcendentals=0),
        name=name,
    )(*operands)


def out(shape, dtype):
    return jax.ShapeDtypeStruct(shape, dtype)


def live_row(waves_ref, first, j):
    lane = lax.broadcasted_iota(jnp.int32, (1, NTOT), 1)
    return (lane >= waves_ref[first + j]).astype(F32)


def fold(first, second, q, m, extra):
    lane = lax.broadcasted_iota(jnp.int32, first.shape, 1)
    turned = pltpu.roll(second, m, axis=1)
    block = lax.broadcasted_iota(jnp.int32, extra.shape, 1)
    extra = jnp.where(block == q, pltpu.roll(turned[:, 128:], q + 1, axis=1), extra)
    return jnp.where(lane >= m, first, turned), extra


def unfold(both, extra, q, m):
    lane = lax.broadcasted_iota(jnp.int32, both.shape, 1)
    block = lax.broadcasted_iota(jnp.int32, extra.shape, 1)
    last = jnp.where(block == 127, pltpu.roll(extra, 127 - q, axis=1), both[:, 128:])
    turned = jnp.concatenate([both[:, :128], last], axis=1)
    turned = pltpu.roll(turned, (NTOT - m) & (NTOT - 1), axis=1)
    return jnp.where(lane >= m, both, 0.0), jnp.where(lane >= NTOT - 1 - m, turned, 0.0)


def pack_state(
    waves_hbm, target_hbm, state_hbm, send_ref, rows_ref, state_ref, waves_ref, target_ref, sems, small_sems
):
    copies = [
        pltpu.make_async_copy(state_hbm.at[j], state_ref.at[j], sems.at[j]) for j in range(SLOTS)
    ]
    waves_copy = pltpu.make_async_copy(waves_hbm, waves_ref, small_sems.at[0])
    target_copy = pltpu.make_async_copy(target_hbm, target_ref, small_sems.at[1])
    for copy in (*copies, waves_copy, target_copy):
        copy.start()
    target_copy.wait()
    waves_copy.wait()
    first = lax.axis_index("wave") * SLOTS
    lane = lax.broadcasted_iota(jnp.int32, (16, 128), 1)
    row = lax.broadcasted_iota(jnp.int32, (16, 128), 0)
    rider = jnp.zeros((16, 128), F32)
    for i in range(ROWL):
        rider = jnp.where((lane == SLOTS // 2) & (row == i), target_ref[i], rider)
    extra = jnp.concatenate([rider] * LEVS, axis=0)
    for q in range(SLOTS // 2):
        for j in (2 * q, 2 * q + 1):
            copies[j].wait()
            for e in range(LEVS):
                for c in range(2):
                    for f in range(2):
                        at = c * 8 + f * 4
                        rows_ref[j, e, at : at + 4, :] = state_ref[j, c, e, f]
        flat = [rows_ref[j].reshape(LEVS * 16, NTOT) for j in (2 * q, 2 * q + 1)]
        both, extra = fold(*flat, q, waves_ref[first + 2 * q], extra)
        send_ref[:, :, q * NTOT : (q + 1) * NTOT] = both.astype(BF16).reshape(LEVS, 16, NTOT)
    send_ref[:, :, 4 * NTOT :] = extra.astype(BF16).reshape(LEVS, 16, 128)


def sine_of(q):
    a = q * (2.0 * math.pi / NLON)
    b = a * a
    total = jnp.full_like(b, -2.5052108e-8)
    for factor in (2.7557319e-6, -1.9841270e-4, 8.3333333e-3, -1.6666667e-1, 1.0):
        total = total * b + factor
    return total * a


def prepare(
    lats_ref, weights_ref, lat_ref, weight_ref, waves_ref, legendre_hbm, w_in_ref, b_in_ref, w_lat_ref, w_mid_ref,
    b_mid_ref, band_ref, const_ref, cos_t_hbm, sin_t_hbm, cos_hbm, sin_hbm, first_hbm, mid_hbm, bias_hbm, scale_hbm,
    hot_ref, cos_t_ref, sin_t_ref, cos_ref, sin_ref, first_ref, mid_ref, bias_ref, scale_ref, legendre_ref, sems, in_sem,
):
    pairs = (
        (cos_t_ref, cos_t_hbm),
        (sin_t_ref, sin_t_hbm),
        (cos_ref, cos_hbm),
        (sin_ref, sin_hbm),
        (first_ref, first_hbm),
        (mid_ref, mid_hbm),
        (bias_ref, bias_hbm),
        (scale_ref, scale_hbm),
    )
    copies = [pltpu.make_async_copy(a, b, sems.at[i]) for i, (a, b) in enumerate(pairs)]
    legendre_copy = pltpu.make_async_copy(legendre_hbm, legendre_ref, in_sem)
    legendre_copy.start()
    x = lax.broadcasted_iota(jnp.int32, (NLON, MW), 0)
    product = (x * waves_ref[...]).astype(F32)
    phase = product - NLON * jnp.floor(product * (1.0 / NLON) + 0.5)
    size = jnp.abs(phase)
    cosine = sine_of(NLON // 4 - size)
    sine = sine_of(jnp.where(size > NLON // 4, jnp.where(phase > 0, 1.0, -1.0) * (NLON // 2) - phase, phase))
    sine = -sine
    cos_t_ref[...] = (cosine * MW**-0.5).astype(BF16)
    copies[0].start()
    sin_t_ref[...] = (sine * MW**-0.5).astype(BF16)
    copies[1].start()
    cos_ref[...] = cosine.T.astype(BF16)
    copies[2].start()
    sin_ref[...] = sine.T.astype(BF16)
    copies[3].start()
    first_ref[...] = jnp.zeros_like(first_ref)
    half_in = (w_in_ref[...].astype(F32) * 0.5).astype(BF16)
    first_ref[0, :FEAT, :] = half_in
    first_ref[1, FEAT:, :] = half_in
    copies[4].start()
    mid_ref[...] = (w_mid_ref[...].astype(F32) * 0.5).astype(BF16)
    copies[5].start()
    lane = lax.broadcasted_iota(jnp.int32, (1, BAND * FEAT), 1)
    scale = jnp.zeros((1, BAND * FEAT), F32)
    own = lax.axis_index("wave") * BAND
    for b in range(BAND):
        t = lats_ref[own + b]
        here = (lane >= b * FEAT) & (lane < (b + 1) * FEAT)
        scale = jnp.where(here, weights_ref[t] * ((2.0 * MW) ** 0.5 / NLON), scale)
        at = jnp.full((1, HID), t, jnp.int32).astype(F32)
        coslat = jnp.sin((at + 0.5) * (math.pi / NLAT))
        bias_ref[b : b + 1, :] = 0.5 * (b_in_ref[...] + coslat * w_lat_ref[...])
    bias_ref[BAND : BAND + 1, :] = 0.5 * b_mid_ref[...]
    copies[6].start()
    scale_ref[...] = scale
    copies[7].start()

    t = lax.broadcasted_iota(jnp.int32, (NLAT, NLAT), 0)
    hot = (t == lat_ref[...]).astype(F32).T
    for i in range(NLAT // 128):
        hot_ref[i] = hot[:, i * 128 : (i + 1) * 128]
    pick = []
    for parity in range(2):
        parts = [
            jnp.concatenate(
                [hot_ref[i, pl.ds(2 * p + parity, WAVES, stride=BAND), :] for p in range(PAIRS)], axis=0
            )
            for i in range(NLAT // 128)
        ]
        pick.append(jnp.concatenate(parts, axis=1).astype(BF16))
    weight = weight_ref[...]
    high = weight.astype(BF16)
    low = (weight - high.astype(F32)).astype(BF16)
    row = lax.broadcasted_iota(jnp.int32, (16, NLAT), 0)
    both = jnp.where(row == 0, high.astype(F32), jnp.where(row == 1, low.astype(F32), 0.0))
    both = both.astype(BF16)
    legendre_copy.wait()
    for j in range(SLOTS):
        block = legendre_ref[j]
        for parity in range(2):
            band_ref[j, :, parity * NTOT : (parity + 1) * NTOT] = jnp.dot(
                pick[parity], block, preferred_element_type=F32
            ).astype(BF16)
        sums = jnp.dot(both, block, preferred_element_type=F32)
        const_ref[j : j + 1, :] = jnp.sum(sums, axis=0, keepdims=True)
    for copy in copies:
        copy.wait()


def to_fourier(
    waves_ref, recv_ref, band_ref, fourier_ref, state_ref, target_ref, rows_ref, both_ref, total_ref
):
    first = lax.axis_index("wave") * SLOTS
    both_ref[...] = jnp.zeros_like(both_ref)
    extra = recv_ref[:, :, 4 * NTOT :].astype(F32)
    for src in range(LEVS):
        at = src * ROWL
        target_ref[at : at + ROWL, :] = jnp.broadcast_to(
            extra[src, :ROWL, SLOTS // 2 : SLOTS // 2 + 1], (ROWL, 128)
        )
    extra = extra.reshape(LEVS * 16, 128)
    for j in range(SLOTS):
        k = j % 2
        q = j // 2
        if k == 0:
            both = recv_ref[:, :, q * NTOT : (q + 1) * NTOT].astype(F32).reshape(LEVS * 16, NTOT)
            split = unfold(both, extra, q, waves_ref[first + j])
        for src in range(LEVS):
            block = split[k][src * 16 : (src + 1) * 16]
            for c in range(2):
                for f in range(2):
                    at = f * LEVELS + src * ROWL
                    rows_ref[k, c, at : at + 4, :] = block[c * 8 + f * 4 : c * 8 + f * 4 + 4, :]
        for c in range(2):
            part = rows_ref[k, c].astype(BF16)
            state_ref[j, c] = part
            both_ref[k, c * 128 : c * 128 + 64, :NTOT] = part
            both_ref[k, c * 128 + 64 : c * 128 + 128, NTOT:] = part
        sums = lax.dot_general(
            band_ref[j], both_ref[k], (((1,), (1,)), ((), ())), preferred_element_type=F32
        )
        for c in range(2):
            for p in range(PAIRS):
                total_ref[c * PAIRS + p, pl.ds(j, WAVES, stride=SLOTS), :] = sums[
                    p * WAVES : (p + 1) * WAVES, c * 128 : (c + 1) * 128
                ]
    for i in range(2 * PAIRS):
        fourier_ref[:, i * 128 : (i + 1) * 128] = total_ref[i].astype(BF16)


def half_silu(u):
    return (u + u * jnp.tanh(u)).astype(BF16)


def dot_lanes(a, b):
    return lax.dot_general(a, b, (((1,), (1,)), ((), ())), preferred_element_type=F32)


def columns(
    coef_ref, cos_t_ref, sin_t_ref, first_ref, bias_ref, mid_ref, last_ref, cos_ref, sin_ref, scale_ref,
    tendw_ref, grid_hbm, values_ref, grid_ref, hidden_ref,
    grid_sems,
):
    def grid_copy(p):
        rows = pl.ds(2 * p, 2)
        return pltpu.make_async_copy(grid_ref.at[rows], grid_hbm.at[rows], grid_sems.at[p])

    half = BAND * FEAT
    values = jnp.dot(cos_t_ref[...], coef_ref[:, :half], preferred_element_type=F32)
    values += jnp.dot(sin_t_ref[...], coef_ref[:, half:], preferred_element_type=F32)
    for p in range(PAIRS):
        values_ref[p] = values[:, p * 128 : (p + 1) * 128].astype(BF16)

    for p in range(PAIRS):
        for q in range(2):
            hidden = jnp.dot(values_ref[p], first_ref[q], preferred_element_type=F32)
            hidden_ref[q, 0] = half_silu(hidden + bias_ref[2 * p + q : 2 * p + q + 1, :])
            hidden = jnp.dot(hidden_ref[q, 0], mid_ref[...], preferred_element_type=F32)
            hidden_ref[q, 1] = half_silu(hidden + bias_ref[BAND : BAND + 1, :])
            grid_ref[2 * p + q] = dot_lanes(last_ref[...], hidden_ref[q, 1]).astype(BF16)
        grid_copy(p).start()
    tend = grid_ref[...].reshape(half, NLON)
    scale = scale_ref[...]
    for c, table in enumerate((cos_ref, sin_ref)):
        tendw_ref[:, c * half : (c + 1) * half] = (dot_lanes(table[...], tend) * scale).astype(BF16)
    for p in range(PAIRS):
        grid_copy(p).wait()


def to_spectral(
    waves_ref, recv_ref, band_ref, state_ref, const_ref, weight_ref, target_ref, coupling_ref,
    send_ref, wide_ref, temp_ref, rows_ref,
):
    first = lax.axis_index("wave") * SLOTS
    for i in range(2 * PAIRS):
        wide_ref[i] = recv_ref[:, i * 128 : (i + 1) * 128].astype(F32)
    target = target_ref[:, :1]
    weight_total = jnp.sum(weight_ref[...], axis=1, keepdims=True)
    degree = lax.broadcasted_iota(jnp.int32, (1, NTOT), 1)
    shrink = 1.0 / (1.0 + diffusion * (degree * (degree + 1)).astype(F32) / (NTOT * NTOT))
    for j in range(SLOTS):
        live = live_row(waves_ref, first, j)
        is_zero = (jnp.full((1, NTOT), waves_ref[first + j], jnp.int32) == 0).astype(F32)
        block = jnp.concatenate(
            [
                jnp.concatenate(
                    [wide_ref[c * PAIRS + p, pl.ds(j, WAVES, stride=SLOTS), :] for c in range(2)],
                    axis=1,
                )
                for p in range(PAIRS)
            ],
            axis=0,
        )
        turned = block.T
        tend_sum = jnp.sum(turned[:128], axis=1, keepdims=True)
        parts = turned.astype(BF16)
        even = jnp.concatenate([parts[:64], parts[128:192]], axis=0)
        odd = jnp.concatenate([parts[64:128], parts[192:]], axis=0)
        spec = jnp.dot(even, band_ref[j, :, :NTOT], preferred_element_type=F32)
        spec += jnp.dot(odd, band_ref[j, :, NTOT:], preferred_element_type=F32)
        const = const_ref[j : j + 1, :]
        for c in range(2):
            old = state_ref[j, c].astype(F32)
            old_temp, old_hum = old[:LEVELS], old[LEVELS:]
            temp = spec[c * 64 : c * 64 + 32]
            hum = spec[c * 64 + 32 : c * 64 + 64]
            if c == 0:
                mean = jnp.sum(old_temp * const, axis=1, keepdims=True)
                mean += time_step * (tend_sum[:32] + tend_sum[64:96])
                nudge = nudge_rate * (target - mean / weight_total)
                temp = temp + nudge * (const * is_zero)
            temp_ref[j * 2 + c] = (old_temp + time_step * temp) * live
            hum = (old_hum + time_step * hum) * (live * shrink)
            for d in range(LEVS):
                rows_ref[j, d, c * 8 + 4 : c * 8 + 8, :] = hum[d * 4 : d * 4 + 4]
    group = 4
    for g in range(2 * SLOTS // group):
        for half in range(2):
            lanes = slice(half * 128, (half + 1) * 128)
            temps = [temp_ref[g * group + i, :, lanes] for i in range(group)]
            for level in range(LEVELS):
                matrix = coupling_ref[level * LEVELS : (level + 1) * LEVELS, lanes]
                for i in range(group):
                    j, c = divmod(g * group + i, 2)
                    at = c * 8 + level % ROWL
                    rows_ref[j, level // ROWL, at : at + 1, lanes] = jnp.sum(
                        matrix * temps[i], axis=0, keepdims=True
                    )
    extra = jnp.zeros((LEVS * 16, 128), F32)
    for q in range(SLOTS // 2):
        flat = [rows_ref[j].reshape(LEVS * 16, NTOT) for j in (2 * q, 2 * q + 1)]
        both, extra = fold(*flat, q, waves_ref[first + 2 * q], extra)
        send_ref[:, :, q * NTOT : (q + 1) * NTOT] = both.astype(BF16).reshape(LEVS, 16, NTOT)
    send_ref[:, :, 4 * NTOT :] = extra.astype(BF16).reshape(LEVS, 16, 128)


def unpack_state(waves_ref, recv_ref, state_hbm, state_ref, sems):
    copies = [
        pltpu.make_async_copy(state_ref.at[j], state_hbm.at[j], sems.at[j]) for j in range(SLOTS)
    ]
    first = lax.axis_index("wave") * SLOTS
    extra = recv_ref[:, :, 4 * NTOT :].astype(F32).reshape(LEVS * 16, 128)
    for q in range(SLOTS // 2):
        both = recv_ref[:, :, q * NTOT : (q + 1) * NTOT].astype(F32).reshape(LEVS * 16, NTOT)
        split = unfold(both, extra, q, waves_ref[first + 2 * q])
        for k in range(2):
            for e in range(LEVS):
                for c in range(2):
                    for f in range(2):
                        at = e * 16 + c * 8 + f * 4
                        state_ref[2 * q + k, c, e, f] = split[k][at : at + 4, :]
            copies[2 * q + k].start()
    for copy in copies:
        copy.wait()


def per_device(
    state,
    wave_table,
    lat_table,
    lat_weight,
    legendre,
    w_in,
    b_in,
    w_lat,
    w_mid,
    b_mid,
    w_out,
    target,
    coupling,
):
    message = (LEVS, 16, SLOTS // 2 * NTOT + 128)
    rows = (SLOTS, LEVS, 16, NTOT)
    sent = call(
        pack_state,
        out(message, BF16),
        [
            pltpu.VMEM(rows, F32),
            pltpu.VMEM(state.shape, F32),
            pltpu.SMEM((MW,), jnp.int32),
            pltpu.SMEM((ROWL,), F32),
            pltpu.SemaphoreType.DMA((SLOTS,)),
            pltpu.SemaphoreType.DMA((2,)),
        ],
        10**8,
        (wave_table, target, state),
        [HBM] * 3,
        "pack_state",
    )
    members = lax.all_to_all(sent, "lev", 0, 0, tiled=True)
    table, turned, weights = (NLON, MW), (MW, NLON), (2, 2 * FEAT, HID)
    made = [
        (table, BF16),
        (table, BF16),
        (turned, BF16),
        (turned, BF16),
        (weights, BF16),
        ((HID, HID), BF16),
        ((16, HID), F32),
        ((1, BAND * FEAT), F32),
    ]
    band, const, cos_t, sin_t, cos, sin, first, mid, bias, scale = call(
        prepare,
        (
            out((SLOTS, PAIRS * WAVES, 2 * NTOT), BF16),
            out((SLOTS, NTOT), F32),
            *(pltpu.HBM(*m) for m in made),
        ),
        [
            pltpu.VMEM((NLAT // 128, NLAT, 128), F32),
            *(pltpu.VMEM(*m) for m in made),
            pltpu.VMEM(legendre.shape, BF16),
            pltpu.SemaphoreType.DMA((len(made),)),
            pltpu.SemaphoreType.DMA,
        ],
        6 * 10**9,
        (
            lat_table,
            lat_weight,
            lat_table[None],
            lat_weight[None],
            wave_table[None],
            legendre,
            w_in,
            b_in[None],
            w_lat[None],
            w_mid,
            b_mid[None],
        ),
        [SMEM] * 2 + [VMEM] * 3 + [HBM] + [VMEM] * 5,
        "prepare",
    )
    fourier, state_bf, target_all = call(
        to_fourier,
        (
            out((MW, 2 * BAND * FEAT), BF16),
            out((SLOTS, 2, FEAT, NTOT), BF16),
            out((LEVELS, 128), F32),
        ),
        [
            pltpu.VMEM((2, 2, FEAT, NTOT), F32),
            pltpu.VMEM((2, NTOT, 2 * NTOT), BF16),
            pltpu.VMEM((2 * PAIRS, MW, 128), F32),
        ],
        10**9,
        (wave_table, members, band),
        [SMEM] + [VMEM] * 2,
        "to_fourier",
    )
    coef = lax.all_to_all(fourier, "wave", 0, 0, tiled=True)
    tendw, grid = call(
        columns,
        (
            out((MW, 2 * BAND * FEAT), BF16),
            pltpu.HBM((BAND, FEAT, NLON), BF16),
        ),
        [
            pltpu.VMEM((PAIRS, NLON, 128), BF16),
            pltpu.VMEM((BAND, FEAT, NLON), BF16),
            pltpu.VMEM((2, 2, NLON, HID), BF16),
            pltpu.SemaphoreType.DMA((PAIRS,)),
        ],
        10**10,
        (coef, cos_t, sin_t, first, bias, mid, w_out.T, cos, sin, scale),
        [VMEM] * 10,
        "columns",
    )
    back = lax.all_to_all(tendw, "wave", 0, 0, tiled=True)
    moved = call(
        to_spectral,
        out(message, BF16),
        [
            pltpu.VMEM((2 * PAIRS, MW, 128), F32),
            pltpu.VMEM((2 * SLOTS, LEVELS, NTOT), F32),
            pltpu.VMEM(rows, F32),
        ],
        10**9,
        (
            wave_table,
            back,
            band,
            state_bf,
            const,
            lat_weight[None],
            target_all,
            jnp.transpose(coupling, (1, 2, 0)).reshape(LEVELS * LEVELS, NTOT),
        ),
        [SMEM] + [VMEM] * 7,
        "to_spectral",
    )
    returned = lax.all_to_all(moved, "lev", 0, 0, tiled=True)
    new_state = call(
        unpack_state,
        pltpu.HBM(state.shape, F32),
        [pltpu.VMEM(state.shape, F32), pltpu.SemaphoreType.DMA((SLOTS,))],
        10**8,
        (wave_table, returned),
        [SMEM, VMEM],
        "unpack_state",
    )
    return new_state, jnp.transpose(grid, (1, 0, 2))[None]


def solution(mesh):
    placed = (
        P("wave", None, None, None, "lev", None),
        P(),
        P(),
        P(),
        P("wave", None, None),
        P(),
        P(),
        P(),
        P(),
        P(),
        P(),
        P("lev"),
        P(),
    )
    return jax.shard_map(
        per_device,
        mesh=mesh,
        in_specs=placed,
        out_specs=(P("wave", None, None, None, "lev", None), P("lev", None, "wave", None)),
        check_vma=False,
    )
```

```python
import math

import jax
import jax.numpy as jnp
from jax import lax
from jax.experimental import pallas as pl
from jax.experimental.pallas import tpu as pltpu
from jax.sharding import PartitionSpec as P

F32 = jnp.float32
BF16 = jnp.bfloat16
WAVES = 32
LEVS = 8
MW = 256
NTOT = 256
NLAT = 384
NLON = 768
HID = 512
SLOTS = MW // WAVES
BAND = NLAT // WAVES
PAIRS = BAND // 2
LEVELS = 32
FEAT = 64
ROWL = LEVELS // LEVS
time_step = 0.5
nudge_rate = 0.5
diffusion = 0.5

VMEM = pl.BlockSpec(memory_space=pltpu.VMEM)
HBM = pl.BlockSpec(memory_space=pltpu.HBM)


def call(body, outs, scratch, flops, operands, specs, name):
    operands = [
        pltpu.with_memory_space_constraint(o, pltpu.HBM) if spec is HBM else o
        for o, spec in zip(operands, specs)
    ]
    return pl.pallas_call(
        body,
        out_shape=outs,
        in_specs=specs,
        out_specs=jax.tree.map(lambda o: HBM if isinstance(o, pl.MemoryRef) else VMEM, outs),
        scratch_shapes=scratch,
        compiler_params=pltpu.CompilerParams(vmem_limit_bytes=40 * 2**20),
        cost_estimate=pl.CostEstimate(flops=flops, bytes_accessed=2 * 10**6, transcendentals=0),
        name=name,
    )(*operands)


def out(shape, dtype):
    return jax.ShapeDtypeStruct(shape, dtype)


def own_waves(waves_ref):
    lane = lax.broadcasted_iota(jnp.int32, (1, MW), 1)
    row = waves_ref[...].astype(F32)
    first = lax.axis_index("wave") * SLOTS
    return [
        jnp.sum(jnp.where(lane == first + 2 * q, row, 0.0)).astype(jnp.int32)
        for q in range(SLOTS // 2)
    ]


def fold(first, second, q, m, extra):
    lane = lax.broadcasted_iota(jnp.int32, first.shape, 1)
    turned = pltpu.roll(second, m, axis=1)
    block = lax.broadcasted_iota(jnp.int32, extra.shape, 1)
    extra = jnp.where(block == q, pltpu.roll(turned[:, 128:], q + 1, axis=1), extra)
    return jnp.where(lane >= m, first, turned), extra


def unfold(both, extra, q, m):
    lane = lax.broadcasted_iota(jnp.int32, both.shape, 1)
    block = lax.broadcasted_iota(jnp.int32, extra.shape, 1)
    last = jnp.where(block == 127, pltpu.roll(extra, 127 - q, axis=1), both[:, 128:])
    turned = jnp.concatenate([both[:, :128], last], axis=1)
    turned = pltpu.roll(turned, (NTOT - m) & (NTOT - 1), axis=1)
    return jnp.where(lane >= m, both, 0.0), jnp.where(lane >= NTOT - 1 - m, turned, 0.0)


def pack_state(
    waves_hbm, target_hbm, state_hbm, send_ref, rows_ref, state_ref, waves_ref, target_ref, sems, small_sems
):
    copies = [
        pltpu.make_async_copy(state_hbm.at[half], state_ref.at[half], sems.at[i])
        for i, half in enumerate((pl.ds(0, SLOTS // 2), pl.ds(SLOTS // 2, SLOTS // 2)))
    ]
    waves_copy = pltpu.make_async_copy(waves_hbm, waves_ref, small_sems.at[0])
    target_copy = pltpu.make_async_copy(target_hbm, target_ref, small_sems.at[1])
    for copy in (*copies, waves_copy, target_copy):
        copy.start()
    target_copy.wait()
    waves_copy.wait()
    first = lax.axis_index("wave") * SLOTS
    lane = lax.broadcasted_iota(jnp.int32, (16, 128), 1)
    row = lax.broadcasted_iota(jnp.int32, (16, 128), 0)
    rider = jnp.zeros((16, 128), F32)
    for i in range(ROWL):
        rider = jnp.where((lane == SLOTS // 2) & (row == i), target_ref[i], rider)
    extra = jnp.concatenate([rider] * LEVS, axis=0)
    for q in range(SLOTS // 2):
        if q % 2 == 0:
            copies[q // 2].wait()
        for j in (2 * q, 2 * q + 1):
            for e in range(LEVS):
                for c in range(2):
                    for f in range(2):
                        at = c * 8 + f * 4
                        rows_ref[j, e, at : at + 4, :] = state_ref[j, c, e, f]
        flat = [rows_ref[j].reshape(LEVS * 16, NTOT) for j in (2 * q, 2 * q + 1)]
        both, extra = fold(*flat, q, waves_ref[first + 2 * q], extra)
        send_ref[:, :, q * NTOT : (q + 1) * NTOT] = both.astype(BF16).reshape(LEVS, 16, NTOT)
    send_ref[:, :, 4 * NTOT :] = extra.astype(BF16).reshape(LEVS, 16, 128)


def sine_of(q):
    a = q * (2.0 * math.pi / NLON)
    b = a * a
    total = jnp.full_like(b, -2.5052108e-8)
    for factor in (2.7557319e-6, -1.9841270e-4, 8.3333333e-3, -1.6666667e-1, 1.0):
        total = total * b + factor
    return total * a


def prepare(
    lats_hbm, weights_hbm, lat_ref, weight_ref, waves_ref, legendre_hbm, w_in_ref, b_in_ref, w_lat_ref, w_mid_ref,
    b_mid_ref, band_ref, const_ref, cos_t_hbm, sin_t_hbm, cos_hbm, sin_hbm, first_hbm, mid_hbm, bias_hbm, scale_hbm,
    hot_ref, cos_t_ref, sin_t_ref, cos_ref, sin_ref, first_ref, mid_ref, bias_ref, scale_ref, legendre_ref, lats_ref, weights_ref,
    sems, in_sems,
):
    pairs = (
        (cos_t_ref, cos_t_hbm),
        (sin_t_ref, sin_t_hbm),
        (cos_ref, cos_hbm),
        (sin_ref, sin_hbm),
        (first_ref, first_hbm),
        (mid_ref, mid_hbm),
        (bias_ref, bias_hbm),
        (scale_ref, scale_hbm),
    )
    copies = [pltpu.make_async_copy(a, b, sems.at[i]) for i, (a, b) in enumerate(pairs)]
    legendre_copy = pltpu.make_async_copy(legendre_hbm, legendre_ref, in_sems.at[0])
    lats_copy = pltpu.make_async_copy(lats_hbm, lats_ref, in_sems.at[1])
    weights_copy = pltpu.make_async_copy(weights_hbm, weights_ref, in_sems.at[2])
    for copy in (lats_copy, weights_copy, legendre_copy):
        copy.start()
    x = lax.broadcasted_iota(jnp.int32, (NLON, MW), 0)
    product = (x * waves_ref[...]).astype(F32)
    phase = product - NLON * jnp.floor(product * (1.0 / NLON) + 0.5)
    size = jnp.abs(phase)
    cosine = sine_of(NLON // 4 - size)
    sine = sine_of(jnp.where(size > NLON // 4, jnp.where(phase > 0, 1.0, -1.0) * (NLON // 2) - phase, phase))
    sine = -sine
    cos_t_ref[...] = (cosine * MW**-0.5).astype(BF16)
    copies[0].start()
    sin_t_ref[...] = (sine * MW**-0.5).astype(BF16)
    copies[1].start()
    cos_ref[...] = cosine.T.astype(BF16)
    copies[2].start()
    sin_ref[...] = sine.T.astype(BF16)
    copies[3].start()
    first_ref[...] = jnp.zeros_like(first_ref)
    half_in = (w_in_ref[...].astype(F32) * 0.5).astype(BF16)
    first_ref[0, :FEAT, :] = half_in
    first_ref[1, FEAT:, :] = half_in
    copies[4].start()
    mid_ref[...] = (w_mid_ref[...].astype(F32) * 0.5).astype(BF16)
    copies[5].start()
    lane = lax.broadcasted_iota(jnp.int32, (1, BAND * FEAT), 1)
    scale = jnp.zeros((1, BAND * FEAT), F32)
    own = lax.axis_index("wave") * BAND
    lats_copy.wait()
    weights_copy.wait()
    for b in range(BAND):
        t = lats_ref[own + b]
        here = (lane >= b * FEAT) & (lane < (b + 1) * FEAT)
        scale = jnp.where(here, weights_ref[t] * ((2.0 * MW) ** 0.5 / NLON), scale)
        at = jnp.full((1, HID), t, jnp.int32).astype(F32)
        coslat = jnp.sin((at + 0.5) * (math.pi / NLAT))
        bias_ref[b : b + 1, :] = 0.5 * (b_in_ref[...] + coslat * w_lat_ref[...])
    bias_ref[BAND : BAND + 1, :] = 0.5 * b_mid_ref[...]
    copies[6].start()
    scale_ref[...] = scale
    copies[7].start()

    t = lax.broadcasted_iota(jnp.int32, (NLAT, NLAT), 0)
    hot = (t == lat_ref[...]).astype(F32).T
    for i in range(NLAT // 128):
        hot_ref[i] = hot[:, i * 128 : (i + 1) * 128]
    pick = []
    for parity in range(2):
        parts = [
            jnp.concatenate(
                [hot_ref[i, pl.ds(2 * p + parity, WAVES, stride=BAND), :] for p in range(PAIRS)], axis=0
            )
            for i in range(NLAT // 128)
        ]
        pick.append(jnp.concatenate(parts, axis=1).astype(BF16))
    weight = weight_ref[...]
    high = weight.astype(BF16)
    low = (weight - high.astype(F32)).astype(BF16)
    row = lax.broadcasted_iota(jnp.int32, (16, NLAT), 0)
    both = jnp.where(row == 0, high.astype(F32), jnp.where(row == 1, low.astype(F32), 0.0))
    both = both.astype(BF16)
    legendre_copy.wait()
    for j in range(SLOTS):
        block = legendre_ref[j]
        for parity in range(2):
            band_ref[j, :, parity * NTOT : (parity + 1) * NTOT] = jnp.dot(
                pick[parity], block, preferred_element_type=F32
            ).astype(BF16)
        sums = jnp.dot(both, block, preferred_element_type=F32)
        const_ref[j : j + 1, :] = jnp.sum(sums, axis=0, keepdims=True)
    for copy in copies:
        copy.wait()


def to_fourier(
    waves_ref, recv_ref, band_ref, fourier_ref, state_ref, target_ref, rows_ref, both_ref, total_ref
):
    waves = own_waves(waves_ref)
    both_ref[...] = jnp.zeros_like(both_ref)
    extra = recv_ref[:, :, 4 * NTOT :].astype(F32)
    for src in range(LEVS):
        at = src * ROWL
        target_ref[at : at + ROWL, :] = jnp.broadcast_to(
            extra[src, :ROWL, SLOTS // 2 : SLOTS // 2 + 1], (ROWL, 128)
        )
    extra = extra.reshape(LEVS * 16, 128)
    for j in range(SLOTS):
        k = j % 2
        q = j // 2
        if k == 0:
            both = recv_ref[:, :, q * NTOT : (q + 1) * NTOT].astype(F32).reshape(LEVS * 16, NTOT)
            split = unfold(both, extra, q, waves[q])
        for src in range(LEVS):
            block = split[k][src * 16 : (src + 1) * 16]
            for c in range(2):
                for f in range(2):
                    at = f * LEVELS + src * ROWL
                    rows_ref[k, c, at : at + 4, :] = block[c * 8 + f * 4 : c * 8 + f * 4 + 4, :]
        for c in range(2):
            part = rows_ref[k, c].astype(BF16)
            state_ref[j, c] = part
            both_ref[k, c * 128 : c * 128 + 64, :NTOT] = part
            both_ref[k, c * 128 + 64 : c * 128 + 128, NTOT:] = part
        sums = lax.dot_general(
            band_ref[j], both_ref[k], (((1,), (1,)), ((), ())), preferred_element_type=F32
        )
        for c in range(2):
            for p in range(PAIRS):
                total_ref[c * PAIRS + p, pl.ds(j, WAVES, stride=SLOTS), :] = sums[
                    p * WAVES : (p + 1) * WAVES, c * 128 : (c + 1) * 128
                ]
    for i in range(2 * PAIRS):
        fourier_ref[:, i * 128 : (i + 1) * 128] = total_ref[i].astype(BF16)


def half_silu(u):
    return (u + u * jnp.tanh(u)).astype(BF16)


def dot_lanes(a, b):
    return lax.dot_general(a, b, (((1,), (1,)), ((), ())), preferred_element_type=F32)


def columns(
    coef_ref, cos_t_ref, sin_t_ref, first_ref, bias_ref, mid_ref, last_ref, cos_ref, sin_ref, scale_ref,
    tendw_ref, grid_hbm, values_ref, grid_ref, hidden_ref,
    grid_sems,
):
    def grid_copy(p):
        rows = pl.ds(2 * p, 2)
        return pltpu.make_async_copy(grid_ref.at[rows], grid_hbm.at[rows], grid_sems.at[p])

    half = BAND * FEAT
    values = jnp.dot(cos_t_ref[...], coef_ref[:, :half], preferred_element_type=F32)
    values += jnp.dot(sin_t_ref[...], coef_ref[:, half:], preferred_element_type=F32)
    for p in range(PAIRS):
        values_ref[p] = values[:, p * 128 : (p + 1) * 128].astype(BF16)

    for p in range(PAIRS):
        for q in range(2):
            hidden = jnp.dot(values_ref[p], first_ref[q], preferred_element_type=F32)
            hidden_ref[q, 0] = half_silu(hidden + bias_ref[2 * p + q : 2 * p + q + 1, :])
            hidden = jnp.dot(hidden_ref[q, 0], mid_ref[...], preferred_element_type=F32)
            hidden_ref[q, 1] = half_silu(hidden + bias_ref[BAND : BAND + 1, :])
            grid_ref[2 * p + q] = dot_lanes(last_ref[...], hidden_ref[q, 1]).astype(BF16)
        grid_copy(p).start()
    tend = grid_ref[...].reshape(half, NLON)
    scale = scale_ref[...]
    for c, table in enumerate((cos_ref, sin_ref)):
        tendw_ref[:, c * half : (c + 1) * half] = (dot_lanes(table[...], tend) * scale).astype(BF16)
    for p in range(PAIRS):
        grid_copy(p).wait()


def to_spectral(
    waves_ref, recv_ref, band_ref, state_ref, const_ref, weight_ref, target_ref, coupling_ref,
    send_ref, wide_ref, temp_ref, rows_ref,
):
    waves = own_waves(waves_ref)
    for i in range(2 * PAIRS):
        wide_ref[i] = recv_ref[:, i * 128 : (i + 1) * 128].astype(F32)
    target = target_ref[:, :1]
    weight_total = jnp.sum(weight_ref[...], axis=1, keepdims=True)
    degree = lax.broadcasted_iota(jnp.int32, (1, NTOT), 1)
    shrink = 1.0 / (1.0 + diffusion * (degree * (degree + 1)).astype(F32) / (NTOT * NTOT))
    for j in range(SLOTS):
        m = waves[j // 2] if j % 2 == 0 else MW - 1 - waves[j // 2]
        live = (degree >= m).astype(F32)
        is_zero = (jnp.full((1, NTOT), m, jnp.int32) == 0).astype(F32)
        block = jnp.concatenate(
            [
                jnp.concatenate(
                    [wide_ref[c * PAIRS + p, pl.ds(j, WAVES, stride=SLOTS), :] for c in range(2)],
                    axis=1,
                )
                for p in range(PAIRS)
            ],
            axis=0,
        )
        turned = block.T
        tend_sum = jnp.sum(turned[:128], axis=1, keepdims=True)
        parts = turned.astype(BF16)
        even = jnp.concatenate([parts[:64], parts[128:192]], axis=0)
        odd = jnp.concatenate([parts[64:128], parts[192:]], axis=0)
        spec = jnp.dot(even, band_ref[j, :, :NTOT], preferred_element_type=F32)
        spec += jnp.dot(odd, band_ref[j, :, NTOT:], preferred_element_type=F32)
        const = const_ref[j : j + 1, :]
        for c in range(2):
            old = state_ref[j, c].astype(F32)
            old_temp, old_hum = old[:LEVELS], old[LEVELS:]
            temp = spec[c * 64 : c * 64 + 32]
            hum = spec[c * 64 + 32 : c * 64 + 64]
            if c == 0:
                mean = jnp.sum(old_temp * const, axis=1, keepdims=True)
                mean += time_step * (tend_sum[:32] + tend_sum[64:96])
                nudge = nudge_rate * (target - mean / weight_total)
                temp = temp + nudge * (const * is_zero)
            temp_ref[j * 2 + c] = (old_temp + time_step * temp) * live
            hum = (old_hum + time_step * hum) * (live * shrink)
            for d in range(LEVS):
                rows_ref[j, d, c * 8 + 4 : c * 8 + 8, :] = hum[d * 4 : d * 4 + 4]
    group = 4
    for g in range(2 * SLOTS // group):
        for half in range(2):
            lanes = slice(half * 128, (half + 1) * 128)
            temps = [temp_ref[g * group + i, :, lanes] for i in range(group)]
            for level in range(LEVELS):
                matrix = coupling_ref[level * LEVELS : (level + 1) * LEVELS, lanes]
                for i in range(group):
                    j, c = divmod(g * group + i, 2)
                    at = c * 8 + level % ROWL
                    rows_ref[j, level // ROWL, at : at + 1, lanes] = jnp.sum(
                        matrix * temps[i], axis=0, keepdims=True
                    )
    extra = jnp.zeros((LEVS * 16, 128), F32)
    for q in range(SLOTS // 2):
        flat = [rows_ref[j].reshape(LEVS * 16, NTOT) for j in (2 * q, 2 * q + 1)]
        both, extra = fold(*flat, q, waves[q], extra)
        send_ref[:, :, q * NTOT : (q + 1) * NTOT] = both.astype(BF16).reshape(LEVS, 16, NTOT)
    send_ref[:, :, 4 * NTOT :] = extra.astype(BF16).reshape(LEVS, 16, 128)


def unpack_state(waves_ref, recv_ref, state_hbm, state_ref, sems):
    copies = [
        pltpu.make_async_copy(
            state_ref.at[pl.ds(2 * q, 2)], state_hbm.at[pl.ds(2 * q, 2)], sems.at[q]
        )
        for q in range(SLOTS // 2)
    ]
    waves = own_waves(waves_ref)
    extra = recv_ref[:, :, 4 * NTOT :].astype(F32).reshape(LEVS * 16, 128)
    for q in range(SLOTS // 2):
        both = recv_ref[:, :, q * NTOT : (q + 1) * NTOT].astype(F32).reshape(LEVS * 16, NTOT)
        split = unfold(both, extra, q, waves[q])
        for k in range(2):
            for e in range(LEVS):
                for c in range(2):
                    for f in range(2):
                        at = e * 16 + c * 8 + f * 4
                        state_ref[2 * q + k, c, e, f] = split[k][at : at + 4, :]
        copies[q].start()
    for copy in copies:
        copy.wait()


def per_device(
    state,
    wave_table,
    lat_table,
    lat_weight,
    legendre,
    w_in,
    b_in,
    w_lat,
    w_mid,
    b_mid,
    w_out,
    target,
    coupling,
):
    message = (LEVS, 16, SLOTS // 2 * NTOT + 128)
    rows = (SLOTS, LEVS, 16, NTOT)
    sent = call(
        pack_state,
        out(message, BF16),
        [
            pltpu.VMEM(rows, F32),
            pltpu.VMEM(state.shape, F32),
            pltpu.SMEM((MW,), jnp.int32),
            pltpu.SMEM((ROWL,), F32),
            pltpu.SemaphoreType.DMA((2,)),
            pltpu.SemaphoreType.DMA((2,)),
        ],
        10**8,
        (wave_table, target, state),
        [HBM] * 3,
        "pack_state",
    )
    members = lax.all_to_all(sent, "lev", 0, 0, tiled=True)
    table, turned, weights = (NLON, MW), (MW, NLON), (2, 2 * FEAT, HID)
    made = [
        (table, BF16),
        (table, BF16),
        (turned, BF16),
        (turned, BF16),
        (weights, BF16),
        ((HID, HID), BF16),
        ((16, HID), F32),
        ((1, BAND * FEAT), F32),
    ]
    band, const, cos_t, sin_t, cos, sin, first, mid, bias, scale = call(
        prepare,
        (
            out((SLOTS, PAIRS * WAVES, 2 * NTOT), BF16),
            out((SLOTS, NTOT), F32),
            *(pltpu.HBM(*m) for m in made),
        ),
        [
            pltpu.VMEM((NLAT // 128, NLAT, 128), F32),
            *(pltpu.VMEM(*m) for m in made),
            pltpu.VMEM(legendre.shape, BF16),
            pltpu.SMEM((NLAT,), jnp.int32),
            pltpu.SMEM((NLAT,), F32),
            pltpu.SemaphoreType.DMA((len(made),)),
            pltpu.SemaphoreType.DMA((3,)),
        ],
        6 * 10**9,
        (
            lat_table,
            lat_weight,
            lat_table[None],
            lat_weight[None],
            wave_table[None],
            legendre,
            w_in,
            b_in[None],
            w_lat[None],
            w_mid,
            b_mid[None],
        ),
        [HBM] * 2 + [VMEM] * 3 + [HBM] + [VMEM] * 5,
        "prepare",
    )
    fourier, state_bf, target_all = call(
        to_fourier,
        (
            out((MW, 2 * BAND * FEAT), BF16),
            out((SLOTS, 2, FEAT, NTOT), BF16),
            out((LEVELS, 128), F32),
        ),
        [
            pltpu.VMEM((2, 2, FEAT, NTOT), F32),
            pltpu.VMEM((2, NTOT, 2 * NTOT), BF16),
            pltpu.VMEM((2 * PAIRS, MW, 128), F32),
        ],
        10**9,
        (wave_table[None], members, band),
        [VMEM] * 3,
        "to_fourier",
    )
    coef = lax.all_to_all(fourier, "wave", 0, 0, tiled=True)
    tendw, grid = call(
        columns,
        (
            out((MW, 2 * BAND * FEAT), BF16),
            pltpu.HBM((BAND, FEAT, NLON), BF16),
        ),
        [
            pltpu.VMEM((PAIRS, NLON, 128), BF16),
            pltpu.VMEM((BAND, FEAT, NLON), BF16),
            pltpu.VMEM((2, 2, NLON, HID), BF16),
            pltpu.SemaphoreType.DMA((PAIRS,)),
        ],
        10**10,
        (coef, cos_t, sin_t, first, bias, mid, w_out.T, cos, sin, scale),
        [VMEM] * 10,
        "columns",
    )
    back = lax.all_to_all(tendw, "wave", 0, 0, tiled=True)
    moved = call(
        to_spectral,
        out(message, BF16),
        [
            pltpu.VMEM((2 * PAIRS, MW, 128), F32),
            pltpu.VMEM((2 * SLOTS, LEVELS, NTOT), F32),
            pltpu.VMEM(rows, F32),
        ],
        10**9,
        (
            wave_table[None],
            back,
            band,
            state_bf,
            const,
            lat_weight[None],
            target_all,
            jnp.transpose(coupling, (1, 2, 0)).reshape(LEVELS * LEVELS, NTOT),
        ),
        [VMEM] * 8,
        "to_spectral",
    )
    returned = lax.all_to_all(moved, "lev", 0, 0, tiled=True)
    new_state = call(
        unpack_state,
        pltpu.HBM(state.shape, F32),
        [pltpu.VMEM(state.shape, F32), pltpu.SemaphoreType.DMA((SLOTS // 2,))],
        10**8,
        (wave_table[None], returned),
        [VMEM] * 2,
        "unpack_state",
    )
    return new_state, jnp.transpose(grid, (1, 0, 2))[None]


def solution(mesh):
    placed = (
        P("wave", None, None, None, "lev", None),
        P(),
        P(),
        P(),
        P("wave", None, None),
        P(),
        P(),
        P(),
        P(),
        P(),
        P(),
        P("lev"),
        P(),
    )
    return jax.shard_map(
        per_device,
        mesh=mesh,
        in_specs=placed,
        out_specs=(P("wave", None, None, None, "lev", None), P("lev", None, "wave", None)),
        check_vma=False,
    )
```

```python
import math

import jax
import jax.numpy as jnp
from jax import lax
from jax.experimental import pallas as pl
from jax.experimental.pallas import tpu as pltpu
from jax.sharding import PartitionSpec as P

F32 = jnp.float32
BF16 = jnp.bfloat16
WAVES = 32
LEVS = 8
MW = 256
NTOT = 256
NLAT = 384
NLON = 768
HID = 512
SLOTS = MW // WAVES
BAND = NLAT // WAVES
PAIRS = BAND // 2
LEVELS = 32
FEAT = 64
ROWL = LEVELS // LEVS
time_step = 0.5
nudge_rate = 0.5
diffusion = 0.5

VMEM = pl.BlockSpec(memory_space=pltpu.VMEM)
HBM = pl.BlockSpec(memory_space=pltpu.HBM)


def call(body, outs, scratch, flops, operands, specs, name):
    operands = [
        pltpu.with_memory_space_constraint(o, pltpu.HBM) if spec is HBM else o
        for o, spec in zip(operands, specs)
    ]
    return pl.pallas_call(
        body,
        out_shape=outs,
        in_specs=specs,
        out_specs=jax.tree.map(lambda o: HBM if isinstance(o, pl.MemoryRef) else VMEM, outs),
        scratch_shapes=scratch,
        compiler_params=pltpu.CompilerParams(vmem_limit_bytes=40 * 2**20),
        cost_estimate=pl.CostEstimate(flops=flops, bytes_accessed=2 * 10**6, transcendentals=0),
        name=name,
    )(*operands)


def out(shape, dtype):
    return jax.ShapeDtypeStruct(shape, dtype)


def own_waves(waves_ref):
    lane = lax.broadcasted_iota(jnp.int32, (1, MW), 1)
    row = waves_ref[...].astype(F32)
    first = lax.axis_index("wave") * SLOTS
    return [
        jnp.sum(jnp.where(lane == first + 2 * q, row, 0.0)).astype(jnp.int32)
        for q in range(SLOTS // 2)
    ]


def fold(first, second, q, m, extra):
    lane = lax.broadcasted_iota(jnp.int32, first.shape, 1)
    turned = pltpu.roll(second, m, axis=1)
    block = lax.broadcasted_iota(jnp.int32, extra.shape, 1)
    extra = jnp.where(block == q, pltpu.roll(turned[:, 128:], q + 1, axis=1), extra)
    return jnp.where(lane >= m, first, turned), extra


def unfold(both, extra, q, m):
    lane = lax.broadcasted_iota(jnp.int32, both.shape, 1)
    block = lax.broadcasted_iota(jnp.int32, extra.shape, 1)
    last = jnp.where(block == 127, pltpu.roll(extra, 127 - q, axis=1), both[:, 128:])
    turned = jnp.concatenate([both[:, :128], last], axis=1)
    turned = pltpu.roll(turned, (NTOT - m) & (NTOT - 1), axis=1)
    return jnp.where(lane >= m, both, 0.0), jnp.where(lane >= NTOT - 1 - m, turned, 0.0)


def pack_state(
    waves_hbm, target_hbm, state_hbm, send_ref, rows_ref, state_ref, waves_ref, target_ref, sems, small_sems
):
    copies = [
        pltpu.make_async_copy(state_hbm.at[half], state_ref.at[half], sems.at[i])
        for i, half in enumerate((pl.ds(0, SLOTS // 2), pl.ds(SLOTS // 2, SLOTS // 2)))
    ]
    waves_copy = pltpu.make_async_copy(waves_hbm, waves_ref, small_sems.at[0])
    target_copy = pltpu.make_async_copy(target_hbm, target_ref, small_sems.at[1])
    for copy in (*copies, waves_copy, target_copy):
        copy.start()
    target_copy.wait()
    waves_copy.wait()
    first = lax.axis_index("wave") * SLOTS
    lane = lax.broadcasted_iota(jnp.int32, (16, 128), 1)
    row = lax.broadcasted_iota(jnp.int32, (16, 128), 0)
    rider = jnp.zeros((16, 128), F32)
    for i in range(ROWL):
        rider = jnp.where((lane == SLOTS // 2) & (row == i), target_ref[i], rider)
    extra = jnp.concatenate([rider] * LEVS, axis=0)
    for q in range(SLOTS // 2):
        if q % 2 == 0:
            copies[q // 2].wait()
        for j in (2 * q, 2 * q + 1):
            for e in range(LEVS):
                for c in range(2):
                    rows_ref[j, e, c * 8 : c * 8 + 8, :] = state_ref[j, c, e].reshape(8, NTOT)
        flat = [rows_ref[j].reshape(LEVS * 16, NTOT) for j in (2 * q, 2 * q + 1)]
        both, extra = fold(*flat, q, waves_ref[first + 2 * q], extra)
        send_ref[:, :, q * NTOT : (q + 1) * NTOT] = both.astype(BF16).reshape(LEVS, 16, NTOT)
    send_ref[:, :, 4 * NTOT :] = extra.astype(BF16).reshape(LEVS, 16, 128)


def sine_of(q):
    a = q * (2.0 * math.pi / NLON)
    b = a * a
    total = jnp.full_like(b, -2.5052108e-8)
    for factor in (2.7557319e-6, -1.9841270e-4, 8.3333333e-3, -1.6666667e-1, 1.0):
        total = total * b + factor
    return total * a


def prepare(
    lats_hbm, weights_hbm, lat_ref, weight_ref, waves_ref, legendre_hbm, coupling_hbm, w_in_ref, b_in_ref, w_lat_ref, w_mid_ref,
    b_mid_ref, band_ref, const_ref, cos_t_hbm, sin_t_hbm, cos_hbm, sin_hbm, first_hbm, mid_hbm, bias_hbm, scale_hbm,
    by_level_hbm, hot_ref, cos_t_ref, sin_t_ref, cos_ref, sin_ref, first_ref, mid_ref, bias_ref, scale_ref, by_level_ref, legendre_ref, lats_ref,
    weights_ref, coupling_ref, sems, in_sems,
):
    pairs = (
        (cos_t_ref, cos_t_hbm),
        (sin_t_ref, sin_t_hbm),
        (cos_ref, cos_hbm),
        (sin_ref, sin_hbm),
        (first_ref, first_hbm),
        (mid_ref, mid_hbm),
        (bias_ref, bias_hbm),
        (scale_ref, scale_hbm),
        (by_level_ref, by_level_hbm),
    )
    copies = [pltpu.make_async_copy(a, b, sems.at[i]) for i, (a, b) in enumerate(pairs)]
    legendre_copy = pltpu.make_async_copy(legendre_hbm, legendre_ref, in_sems.at[0])
    lats_copy = pltpu.make_async_copy(lats_hbm, lats_ref, in_sems.at[1])
    weights_copy = pltpu.make_async_copy(weights_hbm, weights_ref, in_sems.at[2])
    coupling_copies = [
        pltpu.make_async_copy(
            coupling_hbm.at[:, pl.ds(i * 128, 128)], coupling_ref.at[i], in_sems.at[3 + i]
        )
        for i in range(2)
    ]
    for copy in (lats_copy, weights_copy, legendre_copy, *coupling_copies):
        copy.start()
    x = lax.broadcasted_iota(jnp.int32, (NLON, MW), 0)
    product = (x * waves_ref[...]).astype(F32)
    phase = product - NLON * jnp.floor(product * (1.0 / NLON) + 0.5)
    size = jnp.abs(phase)
    cosine = sine_of(NLON // 4 - size)
    sine = sine_of(jnp.where(size > NLON // 4, jnp.where(phase > 0, 1.0, -1.0) * (NLON // 2) - phase, phase))
    sine = -sine
    cos_t_ref[...] = (cosine * MW**-0.5).astype(BF16)
    copies[0].start()
    sin_t_ref[...] = (sine * MW**-0.5).astype(BF16)
    copies[1].start()
    cos_ref[...] = cosine.astype(BF16).T
    copies[2].start()
    sin_ref[...] = sine.astype(BF16).T
    copies[3].start()
    first_ref[...] = jnp.zeros_like(first_ref)
    half_in = (w_in_ref[...].astype(F32) * 0.5).astype(BF16)
    first_ref[0, :FEAT, :] = half_in
    first_ref[1, FEAT:, :] = half_in
    copies[4].start()
    mid_ref[...] = (w_mid_ref[...].astype(F32) * 0.5).astype(BF16)
    copies[5].start()
    lane = lax.broadcasted_iota(jnp.int32, (1, BAND * FEAT), 1)
    scale = jnp.zeros((1, BAND * FEAT), F32)
    own = lax.axis_index("wave") * BAND
    lats_copy.wait()
    weights_copy.wait()
    for b in range(BAND):
        t = lats_ref[own + b]
        here = (lane >= b * FEAT) & (lane < (b + 1) * FEAT)
        scale = jnp.where(here, weights_ref[t] * ((2.0 * MW) ** 0.5 / NLON), scale)
        at = jnp.full((1, HID), t, jnp.int32).astype(F32)
        coslat = jnp.sin((at + 0.5) * (math.pi / NLAT))
        bias_ref[b : b + 1, :] = 0.5 * (b_in_ref[...] + coslat * w_lat_ref[...])
    bias_ref[BAND : BAND + 1, :] = 0.5 * b_mid_ref[...]
    copies[6].start()
    scale_ref[...] = scale
    copies[7].start()

    for i in range(2):
        coupling_copies[i].wait()
        for k in range(LEVELS):
            by_level_ref[k, :, i * 128 : (i + 1) * 128] = coupling_ref[
                i, pl.ds(k, LEVELS, stride=LEVELS), :
            ]
    copies[8].start()

    t = lax.broadcasted_iota(jnp.int32, (NLAT, NLAT), 0)
    hot = (t == lat_ref[...]).astype(F32).T
    for i in range(NLAT // 128):
        hot_ref[i] = hot[:, i * 128 : (i + 1) * 128]
    pick = []
    for parity in range(2):
        parts = [
            jnp.concatenate(
                [hot_ref[i, pl.ds(2 * p + parity, WAVES, stride=BAND), :] for p in range(PAIRS)], axis=0
            )
            for i in range(NLAT // 128)
        ]
        pick.append(jnp.concatenate(parts, axis=1).astype(BF16))
    weight = weight_ref[...]
    high = weight.astype(BF16)
    low = (weight - high.astype(F32)).astype(BF16)
    row = lax.broadcasted_iota(jnp.int32, (16, NLAT), 0)
    both = jnp.where(row == 0, high.astype(F32), jnp.where(row == 1, low.astype(F32), 0.0))
    both = both.astype(BF16)
    legendre_copy.wait()
    for j in range(SLOTS):
        block = legendre_ref[j]
        for parity in range(2):
            band_ref[j, :, parity * NTOT : (parity + 1) * NTOT] = jnp.dot(
                pick[parity], block, preferred_element_type=F32
            ).astype(BF16)
        sums = jnp.dot(both, block, preferred_element_type=F32)
        const_ref[j : j + 1, :] = jnp.sum(sums, axis=0, keepdims=True)
    for copy in copies:
        copy.wait()


def to_fourier(
    waves_ref, recv_ref, band_ref, fourier_ref, state_ref, target_ref, rows_ref, both_ref, total_ref
):
    waves = own_waves(waves_ref)
    both_ref[...] = jnp.zeros_like(both_ref)
    extra = recv_ref[:, :, 4 * NTOT :].astype(F32)
    for src in range(LEVS):
        at = src * ROWL
        target_ref[at : at + ROWL, :] = jnp.broadcast_to(
            extra[src, :ROWL, SLOTS // 2 : SLOTS // 2 + 1], (ROWL, 128)
        )
    extra = extra.reshape(LEVS * 16, 128)
    for j in range(SLOTS):
        k = j % 2
        q = j // 2
        if k == 0:
            both = recv_ref[:, :, q * NTOT : (q + 1) * NTOT].astype(F32).reshape(LEVS * 16, NTOT)
            split = unfold(both, extra, q, waves[q])
        for src in range(LEVS):
            block = split[k][src * 16 : (src + 1) * 16]
            for c in range(2):
                for f in range(2):
                    at = f * LEVELS + src * ROWL
                    rows_ref[k, c, at : at + 4, :] = block[c * 8 + f * 4 : c * 8 + f * 4 + 4, :]
        for c in range(2):
            part = rows_ref[k, c].astype(BF16)
            state_ref[j, c] = part
            both_ref[k, c * 128 : c * 128 + 64, :NTOT] = part
            both_ref[k, c * 128 + 64 : c * 128 + 128, NTOT:] = part
        sums = lax.dot_general(
            band_ref[j], both_ref[k], (((1,), (1,)), ((), ())), preferred_element_type=F32
        )
        for c in range(2):
            for p in range(PAIRS):
                total_ref[c * PAIRS + p, pl.ds(j, WAVES, stride=SLOTS), :] = sums[
                    p * WAVES : (p + 1) * WAVES, c * 128 : (c + 1) * 128
                ]
    for i in range(2 * PAIRS):
        fourier_ref[:, i * 128 : (i + 1) * 128] = total_ref[i].astype(BF16)


def half_silu(u):
    return (u + u * jnp.tanh(u)).astype(BF16)


def dot_lanes(a, b):
    return lax.dot_general(a, b, (((1,), (1,)), ((), ())), preferred_element_type=F32)


def columns(
    coef_ref, cos_t_ref, sin_t_ref, first_ref, bias_ref, mid_ref, last_ref, cos_ref, sin_ref, scale_ref,
    tendw_ref, grid_hbm, values_ref, grid_ref, hidden_ref,
    grid_sems,
):
    def grid_copy(p):
        rows = pl.ds(2 * p, 2)
        return pltpu.make_async_copy(grid_ref.at[rows], grid_hbm.at[rows], grid_sems.at[p])

    half = BAND * FEAT
    values = jnp.dot(cos_t_ref[...], coef_ref[:, :half], preferred_element_type=F32)
    values += jnp.dot(sin_t_ref[...], coef_ref[:, half:], preferred_element_type=F32)
    for p in range(PAIRS):
        values_ref[p] = values[:, p * 128 : (p + 1) * 128].astype(BF16)

    for p in range(PAIRS):
        for q in range(2):
            hidden = jnp.dot(values_ref[p], first_ref[q], preferred_element_type=F32)
            hidden_ref[q, 0] = half_silu(hidden + bias_ref[2 * p + q : 2 * p + q + 1, :])
            hidden = jnp.dot(hidden_ref[q, 0], mid_ref[...], preferred_element_type=F32)
            hidden_ref[q, 1] = half_silu(hidden + bias_ref[BAND : BAND + 1, :])
            grid_ref[2 * p + q] = dot_lanes(last_ref[...], hidden_ref[q, 1]).astype(BF16)
        grid_copy(p).start()
    tend = grid_ref[...].reshape(half, NLON)
    scale = scale_ref[...]
    for c, table in enumerate((cos_ref, sin_ref)):
        tendw_ref[:, c * half : (c + 1) * half] = (dot_lanes(table[...], tend) * scale).astype(BF16)
    for p in range(PAIRS):
        grid_copy(p).wait()


def to_spectral(
    waves_ref, recv_ref, band_ref, state_ref, const_ref, weight_ref, target_ref, coupling_ref,
    send_ref, wide_ref, temp_ref, rows_ref,
):
    waves = own_waves(waves_ref)
    for i in range(2 * PAIRS):
        wide_ref[i] = recv_ref[:, i * 128 : (i + 1) * 128].astype(F32)
    target = target_ref[:, :1]
    weight_total = jnp.sum(weight_ref[...], axis=1, keepdims=True)
    degree = lax.broadcasted_iota(jnp.int32, (1, NTOT), 1)
    shrink = 1.0 / (1.0 + diffusion * (degree * (degree + 1)).astype(F32) / (NTOT * NTOT))
    for j in range(SLOTS):
        m = waves[j // 2] if j % 2 == 0 else MW - 1 - waves[j // 2]
        live = (degree >= m).astype(F32)
        is_zero = (jnp.full((1, NTOT), m, jnp.int32) == 0).astype(F32)
        block = jnp.concatenate(
            [
                jnp.concatenate(
                    [wide_ref[c * PAIRS + p, pl.ds(j, WAVES, stride=SLOTS), :] for c in range(2)],
                    axis=1,
                )
                for p in range(PAIRS)
            ],
            axis=0,
        )
        parts = block.astype(BF16).T
        tend_sum = jnp.sum(parts[:128].astype(F32), axis=1, keepdims=True)
        even = jnp.concatenate([parts[:64], parts[128:192]], axis=0)
        odd = jnp.concatenate([parts[64:128], parts[192:]], axis=0)
        spec = jnp.dot(even, band_ref[j, :, :NTOT], preferred_element_type=F32)
        spec += jnp.dot(odd, band_ref[j, :, NTOT:], preferred_element_type=F32)
        const = const_ref[j : j + 1, :]
        for c in range(2):
            old = state_ref[j, c].astype(F32)
            old_temp, old_hum = old[:LEVELS], old[LEVELS:]
            temp = spec[c * 64 : c * 64 + 32]
            hum = spec[c * 64 + 32 : c * 64 + 64]
            if c == 0:
                mean = jnp.sum(old_temp * const, axis=1, keepdims=True)
                mean += time_step * (tend_sum[:32] + tend_sum[64:96])
                nudge = nudge_rate * (target - mean / weight_total)
                temp = temp + nudge * (const * is_zero)
            temp_ref[j * 2 + c] = (old_temp + time_step * temp) * live
            hum = (old_hum + time_step * hum) * (live * shrink)
            for d in range(LEVS):
                rows_ref[j, d, c * 8 + 4 : c * 8 + 8, :] = hum[d * 4 : d * 4 + 4]
    group = 4
    for g in range(2 * SLOTS // group):
        totals = [0.0] * group
        for k in range(LEVELS):
            matrix = coupling_ref[k]
            for i in range(group):
                totals[i] = totals[i] + matrix * temp_ref[g * group + i, k : k + 1, :]
        for i in range(group):
            j, c = divmod(g * group + i, 2)
            for d in range(LEVS):
                rows_ref[j, d, c * 8 : c * 8 + 4, :] = totals[i][d * 4 : d * 4 + 4]
    extra = jnp.zeros((LEVS * 16, 128), F32)
    for q in range(SLOTS // 2):
        flat = [rows_ref[j].reshape(LEVS * 16, NTOT) for j in (2 * q, 2 * q + 1)]
        both, extra = fold(*flat, q, waves[q], extra)
        send_ref[:, :, q * NTOT : (q + 1) * NTOT] = both.astype(BF16).reshape(LEVS, 16, NTOT)
    send_ref[:, :, 4 * NTOT :] = extra.astype(BF16).reshape(LEVS, 16, 128)


def unpack_state(waves_ref, recv_ref, state_hbm, state_ref, sems):
    copies = [
        pltpu.make_async_copy(
            state_ref.at[pl.ds(2 * q, 2)], state_hbm.at[pl.ds(2 * q, 2)], sems.at[q]
        )
        for q in range(SLOTS // 2)
    ]
    waves = own_waves(waves_ref)
    extra = recv_ref[:, :, 4 * NTOT :].astype(F32).reshape(LEVS * 16, 128)
    for q in range(SLOTS // 2):
        both = recv_ref[:, :, q * NTOT : (q + 1) * NTOT].astype(F32).reshape(LEVS * 16, NTOT)
        split = unfold(both, extra, q, waves[q])
        for k in range(2):
            for e in range(LEVS):
                for c in range(2):
                    for f in range(2):
                        at = e * 16 + c * 8 + f * 4
                        state_ref[2 * q + k, c, e, f] = split[k][at : at + 4, :]
        copies[q].start()
    for copy in copies:
        copy.wait()


def per_device(
    state,
    wave_table,
    lat_table,
    lat_weight,
    legendre,
    w_in,
    b_in,
    w_lat,
    w_mid,
    b_mid,
    w_out,
    target,
    coupling,
):
    message = (LEVS, 16, SLOTS // 2 * NTOT + 128)
    rows = (SLOTS, LEVS, 16, NTOT)
    sent = call(
        pack_state,
        out(message, BF16),
        [
            pltpu.VMEM(rows, F32),
            pltpu.VMEM(state.shape, F32),
            pltpu.SMEM((MW,), jnp.int32),
            pltpu.SMEM((ROWL,), F32),
            pltpu.SemaphoreType.DMA((2,)),
            pltpu.SemaphoreType.DMA((2,)),
        ],
        10**8,
        (wave_table, target, state),
        [HBM] * 3,
        "pack_state",
    )
    members = lax.all_to_all(sent, "lev", 0, 0, tiled=True)
    table, turned, weights = (NLON, MW), (MW, NLON), (2, 2 * FEAT, HID)
    made = [
        (table, BF16),
        (table, BF16),
        (turned, BF16),
        (turned, BF16),
        (weights, BF16),
        ((HID, HID), BF16),
        ((16, HID), F32),
        ((1, BAND * FEAT), F32),
        ((LEVELS, LEVELS, NTOT), F32),
    ]
    band, const, cos_t, sin_t, cos, sin, first, mid, bias, scale, by_level = call(
        prepare,
        (
            out((SLOTS, PAIRS * WAVES, 2 * NTOT), BF16),
            out((SLOTS, NTOT), F32),
            *(pltpu.HBM(*m) for m in made),
        ),
        [
            pltpu.VMEM((NLAT // 128, NLAT, 128), F32),
            *(pltpu.VMEM(*m) for m in made),
            pltpu.VMEM(legendre.shape, BF16),
            pltpu.SMEM((NLAT,), jnp.int32),
            pltpu.SMEM((NLAT,), F32),
            pltpu.VMEM((2, LEVELS * LEVELS, 128), F32),
            pltpu.SemaphoreType.DMA((len(made),)),
            pltpu.SemaphoreType.DMA((5,)),
        ],
        6 * 10**9,
        (
            lat_table,
            lat_weight,
            lat_table[None],
            lat_weight[None],
            wave_table[None],
            legendre,
            jnp.transpose(coupling, (1, 2, 0)).reshape(LEVELS * LEVELS, NTOT),
            w_in,
            b_in[None],
            w_lat[None],
            w_mid,
            b_mid[None],
        ),
        [HBM] * 2 + [VMEM] * 3 + [HBM] * 2 + [VMEM] * 5,
        "prepare",
    )
    fourier, state_bf, target_all = call(
        to_fourier,
        (
            out((MW, 2 * BAND * FEAT), BF16),
            out((SLOTS, 2, FEAT, NTOT), BF16),
            out((LEVELS, 128), F32),
        ),
        [
            pltpu.VMEM((2, 2, FEAT, NTOT), F32),
            pltpu.VMEM((2, NTOT, 2 * NTOT), BF16),
            pltpu.VMEM((2 * PAIRS, MW, 128), F32),
        ],
        10**9,
        (wave_table[None], members, band),
        [VMEM] * 3,
        "to_fourier",
    )
    coef = lax.all_to_all(fourier, "wave", 0, 0, tiled=True)
    tendw, grid = call(
        columns,
        (
            out((MW, 2 * BAND * FEAT), BF16),
            pltpu.HBM((BAND, FEAT, NLON), BF16),
        ),
        [
            pltpu.VMEM((PAIRS, NLON, 128), BF16),
            pltpu.VMEM((BAND, FEAT, NLON), BF16),
            pltpu.VMEM((2, 2, NLON, HID), BF16),
            pltpu.SemaphoreType.DMA((PAIRS,)),
        ],
        10**10,
        (coef, cos_t, sin_t, first, bias, mid, w_out.T, cos, sin, scale),
        [VMEM] * 10,
        "columns",
    )
    back = lax.all_to_all(tendw, "wave", 0, 0, tiled=True)
    moved = call(
        to_spectral,
        out(message, BF16),
        [
            pltpu.VMEM((2 * PAIRS, MW, 128), F32),
            pltpu.VMEM((2 * SLOTS, LEVELS, NTOT), F32),
            pltpu.VMEM(rows, F32),
        ],
        10**9,
        (
            wave_table[None],
            back,
            band,
            state_bf,
            const,
            lat_weight[None],
            target_all,
            by_level,
        ),
        [VMEM] * 8,
        "to_spectral",
    )
    returned = lax.all_to_all(moved, "lev", 0, 0, tiled=True)
    new_state = call(
        unpack_state,
        pltpu.HBM(state.shape, F32),
        [pltpu.VMEM(state.shape, F32), pltpu.SemaphoreType.DMA((SLOTS // 2,))],
        10**8,
        (wave_table[None], returned),
        [VMEM] * 2,
        "unpack_state",
    )
    return new_state, jnp.transpose(grid, (1, 0, 2))[None]


def solution(mesh):
    placed = (
        P("wave", None, None, None, "lev", None),
        P(),
        P(),
        P(),
        P("wave", None, None),
        P(),
        P(),
        P(),
        P(),
        P(),
        P(),
        P("lev"),
        P(),
    )
    return jax.shard_map(
        per_device,
        mesh=mesh,
        in_specs=placed,
        out_specs=(P("wave", None, None, None, "lev", None), P("lev", None, "wave", None)),
        check_vma=False,
    )
```

```python
import math

import jax
import jax.numpy as jnp
from jax import lax
from jax.experimental import pallas as pl
from jax.experimental.pallas import tpu as pltpu
from jax.sharding import PartitionSpec as P

F32 = jnp.float32
BF16 = jnp.bfloat16
WAVES = 32
LEVS = 8
MW = 256
NTOT = 256
NLAT = 384
NLON = 768
HID = 512
SLOTS = MW // WAVES
BAND = NLAT // WAVES
PAIRS = BAND // 2
LEVELS = 32
FEAT = 64
ROWL = LEVELS // LEVS
time_step = 0.5
nudge_rate = 0.5
diffusion = 0.5

VMEM = pl.BlockSpec(memory_space=pltpu.VMEM)
HBM = pl.BlockSpec(memory_space=pltpu.HBM)


def call(body, outs, scratch, flops, operands, specs, name):
    operands = [
        pltpu.with_memory_space_constraint(o, pltpu.HBM) if spec is HBM else o
        for o, spec in zip(operands, specs)
    ]
    return pl.pallas_call(
        body,
        out_shape=outs,
        in_specs=specs,
        out_specs=jax.tree.map(lambda o: HBM if isinstance(o, pl.MemoryRef) else VMEM, outs),
        scratch_shapes=scratch,
        compiler_params=pltpu.CompilerParams(vmem_limit_bytes=40 * 2**20),
        cost_estimate=pl.CostEstimate(flops=flops, bytes_accessed=2 * 10**6, transcendentals=0),
        name=name,
    )(*operands)


def out(shape, dtype):
    return jax.ShapeDtypeStruct(shape, dtype)


def own_waves(waves_ref):
    lane = lax.broadcasted_iota(jnp.int32, (1, MW), 1)
    row = waves_ref[...].astype(F32)
    first = lax.axis_index("wave") * SLOTS
    return [
        jnp.sum(jnp.where(lane == first + 2 * q, row, 0.0)).astype(jnp.int32)
        for q in range(SLOTS // 2)
    ]


def fold(first, second, q, m, extra):
    lane = lax.broadcasted_iota(jnp.int32, first.shape, 1)
    turned = pltpu.roll(second, m, axis=1)
    block = lax.broadcasted_iota(jnp.int32, extra.shape, 1)
    extra = jnp.where(block == q, pltpu.roll(turned[:, 128:], q + 1, axis=1), extra)
    return jnp.where(lane >= m, first, turned), extra


def unfold(both, extra, q, m):
    lane = lax.broadcasted_iota(jnp.int32, both.shape, 1)
    block = lax.broadcasted_iota(jnp.int32, extra.shape, 1)
    last = jnp.where(block == 127, pltpu.roll(extra, 127 - q, axis=1), both[:, 128:])
    turned = jnp.concatenate([both[:, :128], last], axis=1)
    turned = pltpu.roll(turned, (NTOT - m) & (NTOT - 1), axis=1)
    return jnp.where(lane >= m, both, 0.0), jnp.where(lane >= NTOT - 1 - m, turned, 0.0)


def pack_state(
    waves_hbm, target_hbm, state_hbm, send_ref, rows_ref, state_ref, waves_ref, target_ref, sems, small_sems
):
    copies = [
        pltpu.make_async_copy(state_hbm.at[half], state_ref.at[half], sems.at[i])
        for i, half in enumerate((pl.ds(0, SLOTS // 2), pl.ds(SLOTS // 2, SLOTS // 2)))
    ]
    waves_copy = pltpu.make_async_copy(waves_hbm, waves_ref, small_sems.at[0])
    target_copy = pltpu.make_async_copy(target_hbm, target_ref, small_sems.at[1])
    for copy in (*copies, waves_copy, target_copy):
        copy.start()
    target_copy.wait()
    waves_copy.wait()
    first = lax.axis_index("wave") * SLOTS
    lane = lax.broadcasted_iota(jnp.int32, (16, 128), 1)
    row = lax.broadcasted_iota(jnp.int32, (16, 128), 0)
    rider = jnp.zeros((16, 128), F32)
    for i in range(ROWL):
        rider = jnp.where((lane == SLOTS // 2) & (row == i), target_ref[i], rider)
    extra = jnp.concatenate([rider] * LEVS, axis=0)
    for q in range(SLOTS // 2):
        if q % 2 == 0:
            copies[q // 2].wait()
        for j in (2 * q, 2 * q + 1):
            for e in range(LEVS):
                for c in range(2):
                    rows_ref[j, e, c * 8 : c * 8 + 8, :] = state_ref[j, c, e].reshape(8, NTOT)
        flat = [rows_ref[j].reshape(LEVS * 16, NTOT) for j in (2 * q, 2 * q + 1)]
        both, extra = fold(*flat, q, waves_ref[first + 2 * q], extra)
        send_ref[:, :, q * NTOT : (q + 1) * NTOT] = both.astype(BF16).reshape(LEVS, 16, NTOT)
    send_ref[:, :, 4 * NTOT :] = extra.astype(BF16).reshape(LEVS, 16, 128)


def sine_of(q):
    a = q * (2.0 * math.pi / NLON)
    b = a * a
    total = jnp.full_like(b, -2.5052108e-8)
    for factor in (2.7557319e-6, -1.9841270e-4, 8.3333333e-3, -1.6666667e-1, 1.0):
        total = total * b + factor
    return total * a


def prepare(
    lats_hbm, weights_hbm, lat_ref, weight_ref, waves_ref, legendre_hbm, coupling_hbm, w_in_ref, b_in_ref, w_lat_ref, w_mid_ref,
    b_mid_ref, band_ref, const_ref, cos_t_hbm, sin_t_hbm, cos_hbm, sin_hbm, first_hbm, mid_hbm, bias_hbm, scale_hbm,
    by_level_hbm, hot_ref, cos_t_ref, sin_t_ref, cos_ref, sin_ref, first_ref, mid_ref, bias_ref, scale_ref, by_level_ref, legendre_ref, lats_ref,
    weights_ref, coupling_ref, sems, in_sems,
):
    pairs = (
        (cos_t_ref, cos_t_hbm),
        (sin_t_ref, sin_t_hbm),
        (cos_ref, cos_hbm),
        (sin_ref, sin_hbm),
        (first_ref, first_hbm),
        (mid_ref, mid_hbm),
        (bias_ref, bias_hbm),
        (scale_ref, scale_hbm),
        (by_level_ref, by_level_hbm),
    )
    copies = [pltpu.make_async_copy(a, b, sems.at[i]) for i, (a, b) in enumerate(pairs)]
    legendre_copy = pltpu.make_async_copy(legendre_hbm, legendre_ref, in_sems.at[0])
    lats_copy = pltpu.make_async_copy(lats_hbm, lats_ref, in_sems.at[1])
    weights_copy = pltpu.make_async_copy(weights_hbm, weights_ref, in_sems.at[2])
    coupling_copies = [
        pltpu.make_async_copy(
            coupling_hbm.at[:, pl.ds(i * 128, 128)], coupling_ref.at[i], in_sems.at[3 + i]
        )
        for i in range(2)
    ]
    for copy in (lats_copy, weights_copy, legendre_copy, *coupling_copies):
        copy.start()
    x = lax.broadcasted_iota(jnp.int32, (NLON, MW), 0)
    product = (x * waves_ref[...]).astype(F32)
    phase = product - NLON * jnp.floor(product * (1.0 / NLON) + 0.5)
    size = jnp.abs(phase)
    cosine = sine_of(NLON // 4 - size)
    sine = sine_of(jnp.where(size > NLON // 4, jnp.where(phase > 0, 1.0, -1.0) * (NLON // 2) - phase, phase))
    sine = -sine
    cos_t_ref[...] = (cosine * MW**-0.5).astype(BF16)
    copies[0].start()
    sin_t_ref[...] = (sine * MW**-0.5).astype(BF16)
    copies[1].start()
    cos_ref[...] = cosine.astype(BF16).T
    copies[2].start()
    sin_ref[...] = sine.astype(BF16).T
    copies[3].start()
    first_ref[...] = jnp.zeros_like(first_ref)
    half_in = (w_in_ref[...].astype(F32) * 0.5).astype(BF16)
    first_ref[0, :FEAT, :] = half_in
    first_ref[1, FEAT:, :] = half_in
    copies[4].start()
    mid_ref[...] = (w_mid_ref[...].astype(F32) * 0.5).astype(BF16)
    copies[5].start()
    lane = lax.broadcasted_iota(jnp.int32, (1, BAND * FEAT), 1)
    scale = jnp.zeros((1, BAND * FEAT), F32)
    own = lax.axis_index("wave") * BAND
    lats_copy.wait()
    weights_copy.wait()
    for b in range(BAND):
        t = lats_ref[own + b]
        here = (lane >= b * FEAT) & (lane < (b + 1) * FEAT)
        scale = jnp.where(here, weights_ref[t] * ((2.0 * MW) ** 0.5 / NLON), scale)
        at = jnp.full((1, HID), t, jnp.int32).astype(F32)
        coslat = jnp.sin((at + 0.5) * (math.pi / NLAT))
        bias_ref[b : b + 1, :] = 0.5 * (b_in_ref[...] + coslat * w_lat_ref[...])
    bias_ref[BAND : BAND + 1, :] = 0.5 * b_mid_ref[...]
    copies[6].start()
    scale_ref[...] = scale
    copies[7].start()

    for i in range(2):
        coupling_copies[i].wait()
        for k in range(LEVELS):
            by_level_ref[k, :, i * 128 : (i + 1) * 128] = coupling_ref[
                i, pl.ds(k, LEVELS, stride=LEVELS), :
            ]
    copies[8].start()

    t = lax.broadcasted_iota(jnp.int32, (NLAT, NLAT), 0)
    hot = (t == lat_ref[...]).astype(F32).T
    for i in range(NLAT // 128):
        hot_ref[i] = hot[:, i * 128 : (i + 1) * 128]
    pick = []
    for parity in range(2):
        parts = [
            jnp.concatenate(
                [hot_ref[i, pl.ds(2 * p + parity, WAVES, stride=BAND), :] for p in range(PAIRS)], axis=0
            )
            for i in range(NLAT // 128)
        ]
        pick.append(jnp.concatenate(parts, axis=1).astype(BF16))
    weight = weight_ref[...]
    high = weight.astype(BF16)
    low = (weight - high.astype(F32)).astype(BF16)
    row = lax.broadcasted_iota(jnp.int32, (16, NLAT), 0)
    both = jnp.where(row == 0, high.astype(F32), jnp.where(row == 1, low.astype(F32), 0.0))
    both = both.astype(BF16)
    legendre_copy.wait()
    for j in range(SLOTS):
        block = legendre_ref[j]
        for parity in range(2):
            band_ref[j, :, parity * NTOT : (parity + 1) * NTOT] = jnp.dot(
                pick[parity], block, preferred_element_type=F32
            ).astype(BF16)
        sums = jnp.dot(both, block, preferred_element_type=F32)
        const_ref[j : j + 1, :] = jnp.sum(sums, axis=0, keepdims=True)
    for copy in copies:
        copy.wait()


def to_fourier(
    waves_ref, recv_ref, band_ref, fourier_ref, state_ref, target_ref, rows_ref, both_ref, total_ref
):
    waves = own_waves(waves_ref)
    both_ref[...] = jnp.zeros_like(both_ref)
    extra = recv_ref[:, :, 4 * NTOT :].astype(F32)
    for src in range(LEVS):
        at = src * ROWL
        target_ref[at : at + ROWL, :] = jnp.broadcast_to(
            extra[src, :ROWL, SLOTS // 2 : SLOTS // 2 + 1], (ROWL, 128)
        )
    extra = extra.reshape(LEVS * 16, 128)
    for j in range(SLOTS):
        k = j % 2
        q = j // 2
        if k == 0:
            both = recv_ref[:, :, q * NTOT : (q + 1) * NTOT].astype(F32).reshape(LEVS * 16, NTOT)
            split = unfold(both, extra, q, waves[q])
        for src in range(LEVS):
            block = split[k][src * 16 : (src + 1) * 16]
            for c in range(2):
                for f in range(2):
                    at = f * LEVELS + src * ROWL
                    rows_ref[k, c, at : at + 4, :] = block[c * 8 + f * 4 : c * 8 + f * 4 + 4, :]
        for c in range(2):
            part = rows_ref[k, c].astype(BF16)
            state_ref[j, c] = part
            both_ref[k, c * 128 : c * 128 + 64, :NTOT] = part
            both_ref[k, c * 128 + 64 : c * 128 + 128, NTOT:] = part
        sums = lax.dot_general(
            band_ref[j], both_ref[k], (((1,), (1,)), ((), ())), preferred_element_type=F32
        )
        for c in range(2):
            for p in range(PAIRS):
                total_ref[c * PAIRS + p, pl.ds(j, WAVES, stride=SLOTS), :] = sums[
                    p * WAVES : (p + 1) * WAVES, c * 128 : (c + 1) * 128
                ]
    for i in range(2 * PAIRS):
        fourier_ref[:, i * 128 : (i + 1) * 128] = total_ref[i].astype(BF16)


def half_silu(u):
    return (u + u * jnp.tanh(u)).astype(BF16)


def dot_lanes(a, b):
    return lax.dot_general(a, b, (((1,), (1,)), ((), ())), preferred_element_type=F32)


def columns(
    coef_ref, cos_t_ref, sin_t_ref, first_ref, bias_ref, mid_ref, last_ref, cos_ref, sin_ref, scale_ref,
    tendw_ref, grid_hbm, values_ref, grid_ref, hidden_ref,
    grid_sems,
):
    def grid_copy(p):
        rows = pl.ds(2 * p, 2)
        return pltpu.make_async_copy(grid_ref.at[rows], grid_hbm.at[rows], grid_sems.at[p])

    half = BAND * FEAT
    values = jnp.dot(cos_t_ref[...], coef_ref[:, :half], preferred_element_type=F32)
    values += jnp.dot(sin_t_ref[...], coef_ref[:, half:], preferred_element_type=F32)
    for p in range(PAIRS):
        values_ref[p] = values[:, p * 128 : (p + 1) * 128].astype(BF16)

    for p in range(PAIRS):
        for q in range(2):
            hidden = jnp.dot(values_ref[p], first_ref[q], preferred_element_type=F32)
            hidden_ref[q, 0] = half_silu(hidden + bias_ref[2 * p + q : 2 * p + q + 1, :])
            hidden = jnp.dot(hidden_ref[q, 0], mid_ref[...], preferred_element_type=F32)
            hidden_ref[q, 1] = half_silu(hidden + bias_ref[BAND : BAND + 1, :])
            grid_ref[2 * p + q] = dot_lanes(last_ref[...], hidden_ref[q, 1]).astype(BF16)
        grid_copy(p).start()
    tend = grid_ref[...].reshape(half, NLON)
    scale = scale_ref[...]
    for c, table in enumerate((cos_ref, sin_ref)):
        tendw_ref[:, c * half : (c + 1) * half] = (dot_lanes(table[...], tend) * scale).astype(BF16)
    for p in range(PAIRS):
        grid_copy(p).wait()


def to_spectral(
    waves_ref, recv_ref, band_ref, state_ref, const_ref, weight_ref, target_ref, coupling_ref,
    send_ref, wide_ref, temp_ref, rows_ref, low_ref,
):
    waves = own_waves(waves_ref)
    for i in range(2 * PAIRS):
        wide_ref[i] = recv_ref[:, i * 128 : (i + 1) * 128].astype(F32)
    target = target_ref[:, :1]
    weight_total = jnp.sum(weight_ref[...], axis=1, keepdims=True)
    degree = lax.broadcasted_iota(jnp.int32, (1, NTOT), 1)
    shrink = 1.0 / (1.0 + diffusion * (degree * (degree + 1)).astype(F32) / (NTOT * NTOT))
    for j in range(SLOTS):
        m = waves[j // 2] if j % 2 == 0 else MW - 1 - waves[j // 2]
        live = (degree >= m).astype(F32)
        is_zero = (jnp.full((1, NTOT), m, jnp.int32) == 0).astype(F32)
        block = jnp.concatenate(
            [
                jnp.concatenate(
                    [wide_ref[c * PAIRS + p, pl.ds(j, WAVES, stride=SLOTS), :] for c in range(2)],
                    axis=1,
                )
                for p in range(PAIRS)
            ],
            axis=0,
        )
        parts = block.astype(BF16).T
        tend_sum = jnp.sum(parts[:128].astype(F32), axis=1, keepdims=True)
        even = jnp.concatenate([parts[:64], parts[128:192]], axis=0)
        odd = jnp.concatenate([parts[64:128], parts[192:]], axis=0)
        spec = jnp.dot(even, band_ref[j, :, :NTOT], preferred_element_type=F32)
        spec += jnp.dot(odd, band_ref[j, :, NTOT:], preferred_element_type=F32)
        const = const_ref[j : j + 1, :]
        for c in range(2):
            old = state_ref[j, c].astype(F32)
            old_temp, old_hum = old[:LEVELS], old[LEVELS:]
            temp = spec[c * 64 : c * 64 + 32]
            hum = spec[c * 64 + 32 : c * 64 + 64]
            if c == 0:
                mean = jnp.sum(old_temp * const, axis=1, keepdims=True)
                mean += time_step * (tend_sum[:32] + tend_sum[64:96])
                nudge = nudge_rate * (target - mean / weight_total)
                temp = temp + nudge * (const * is_zero)
            temp_ref[j * 2 + c] = (old_temp + time_step * temp) * live
            hum = (old_hum + time_step * hum) * (live * shrink)
            for d in range(LEVS):
                rows_ref[j, d, c * 8 + 4 : c * 8 + 8, :] = hum[d * 4 : d * 4 + 4]
    for i in range(SLOTS):
        at = i // 2 * 4 + i % 2
        low_ref[i] = temp_ref[at, :, :128] + temp_ref[at + 2, :, :128]
    group = 8
    for g in range(3):
        lanes = slice(0, 128) if g == 2 else slice(128, NTOT)
        totals = [0.0] * group
        for k in range(LEVELS):
            matrix = coupling_ref[k, :, lanes]
            for i in range(group):
                if g == 2:
                    temp = low_ref[i, k : k + 1, :]
                else:
                    temp = temp_ref[g * group + i, k : k + 1, lanes]
                totals[i] = totals[i] + matrix * temp
        for i in range(group):
            if g == 2:
                q, c = divmod(i, 2)
                low = jnp.full((LEVELS, 128), waves[q], jnp.int32) < 128
                parts = [
                    (2 * q, jnp.where(low, totals[i], 0.0)),
                    (2 * q + 1, jnp.where(low, 0.0, totals[i])),
                ]
            else:
                j, c = divmod(g * group + i, 2)
                parts = [(j, totals[i])]
            for j, part in parts:
                for d in range(LEVS):
                    rows_ref[j, d, c * 8 : c * 8 + 4, lanes] = part[d * 4 : d * 4 + 4]
    extra = jnp.zeros((LEVS * 16, 128), F32)
    for q in range(SLOTS // 2):
        flat = [rows_ref[j].reshape(LEVS * 16, NTOT) for j in (2 * q, 2 * q + 1)]
        both, extra = fold(*flat, q, waves[q], extra)
        send_ref[:, :, q * NTOT : (q + 1) * NTOT] = both.astype(BF16).reshape(LEVS, 16, NTOT)
    send_ref[:, :, 4 * NTOT :] = extra.astype(BF16).reshape(LEVS, 16, 128)


def unpack_state(waves_ref, recv_ref, state_hbm, state_ref, sems):
    copies = [
        pltpu.make_async_copy(
            state_ref.at[pl.ds(2 * q, 2)], state_hbm.at[pl.ds(2 * q, 2)], sems.at[q]
        )
        for q in range(SLOTS // 2)
    ]
    waves = own_waves(waves_ref)
    extra = recv_ref[:, :, 4 * NTOT :].astype(F32).reshape(LEVS * 16, 128)
    for q in range(SLOTS // 2):
        both = recv_ref[:, :, q * NTOT : (q + 1) * NTOT].astype(F32).reshape(LEVS * 16, NTOT)
        split = unfold(both, extra, q, waves[q])
        for k in range(2):
            for e in range(LEVS):
                for c in range(2):
                    for f in range(2):
                        at = e * 16 + c * 8 + f * 4
                        state_ref[2 * q + k, c, e, f] = split[k][at : at + 4, :]
        copies[q].start()
    for copy in copies:
        copy.wait()


def per_device(
    state,
    wave_table,
    lat_table,
    lat_weight,
    legendre,
    w_in,
    b_in,
    w_lat,
    w_mid,
    b_mid,
    w_out,
    target,
    coupling,
):
    message = (LEVS, 16, SLOTS // 2 * NTOT + 128)
    rows = (SLOTS, LEVS, 16, NTOT)
    sent = call(
        pack_state,
        out(message, BF16),
        [
            pltpu.VMEM(rows, F32),
            pltpu.VMEM(state.shape, F32),
            pltpu.SMEM((MW,), jnp.int32),
            pltpu.SMEM((ROWL,), F32),
            pltpu.SemaphoreType.DMA((2,)),
            pltpu.SemaphoreType.DMA((2,)),
        ],
        10**8,
        (wave_table, target, state),
        [HBM] * 3,
        "pack_state",
    )
    members = lax.all_to_all(sent, "lev", 0, 0, tiled=True)
    table, turned, weights = (NLON, MW), (MW, NLON), (2, 2 * FEAT, HID)
    made = [
        (table, BF16),
        (table, BF16),
        (turned, BF16),
        (turned, BF16),
        (weights, BF16),
        ((HID, HID), BF16),
        ((16, HID), F32),
        ((1, BAND * FEAT), F32),
        ((LEVELS, LEVELS, NTOT), F32),
    ]
    band, const, cos_t, sin_t, cos, sin, first, mid, bias, scale, by_level = call(
        prepare,
        (
            out((SLOTS, PAIRS * WAVES, 2 * NTOT), BF16),
            out((SLOTS, NTOT), F32),
            *(pltpu.HBM(*m) for m in made),
        ),
        [
            pltpu.VMEM((NLAT // 128, NLAT, 128), F32),
            *(pltpu.VMEM(*m) for m in made),
            pltpu.VMEM(legendre.shape, BF16),
            pltpu.SMEM((NLAT,), jnp.int32),
            pltpu.SMEM((NLAT,), F32),
            pltpu.VMEM((2, LEVELS * LEVELS, 128), F32),
            pltpu.SemaphoreType.DMA((len(made),)),
            pltpu.SemaphoreType.DMA((5,)),
        ],
        6 * 10**9,
        (
            lat_table,
            lat_weight,
            lat_table[None],
            lat_weight[None],
            wave_table[None],
            legendre,
            jnp.transpose(coupling, (1, 2, 0)).reshape(LEVELS * LEVELS, NTOT),
            w_in,
            b_in[None],
            w_lat[None],
            w_mid,
            b_mid[None],
        ),
        [HBM] * 2 + [VMEM] * 3 + [HBM] * 2 + [VMEM] * 5,
        "prepare",
    )
    fourier, state_bf, target_all = call(
        to_fourier,
        (
            out((MW, 2 * BAND * FEAT), BF16),
            out((SLOTS, 2, FEAT, NTOT), BF16),
            out((LEVELS, 128), F32),
        ),
        [
            pltpu.VMEM((2, 2, FEAT, NTOT), F32),
            pltpu.VMEM((2, NTOT, 2 * NTOT), BF16),
            pltpu.VMEM((2 * PAIRS, MW, 128), F32),
        ],
        10**9,
        (wave_table[None], members, band),
        [VMEM] * 3,
        "to_fourier",
    )
    coef = lax.all_to_all(fourier, "wave", 0, 0, tiled=True)
    tendw, grid = call(
        columns,
        (
            out((MW, 2 * BAND * FEAT), BF16),
            pltpu.HBM((BAND, FEAT, NLON), BF16),
        ),
        [
            pltpu.VMEM((PAIRS, NLON, 128), BF16),
            pltpu.VMEM((BAND, FEAT, NLON), BF16),
            pltpu.VMEM((2, 2, NLON, HID), BF16),
            pltpu.SemaphoreType.DMA((PAIRS,)),
        ],
        10**10,
        (coef, cos_t, sin_t, first, bias, mid, w_out.T, cos, sin, scale),
        [VMEM] * 10,
        "columns",
    )
    back = lax.all_to_all(tendw, "wave", 0, 0, tiled=True)
    moved = call(
        to_spectral,
        out(message, BF16),
        [
            pltpu.VMEM((2 * PAIRS, MW, 128), F32),
            pltpu.VMEM((2 * SLOTS, LEVELS, NTOT), F32),
            pltpu.VMEM(rows, F32),
            pltpu.VMEM((SLOTS, LEVELS, 128), F32),
        ],
        10**9,
        (
            wave_table[None],
            back,
            band,
            state_bf,
            const,
            lat_weight[None],
            target_all,
            by_level,
        ),
        [VMEM] * 8,
        "to_spectral",
    )
    returned = lax.all_to_all(moved, "lev", 0, 0, tiled=True)
    new_state = call(
        unpack_state,
        pltpu.HBM(state.shape, F32),
        [pltpu.VMEM(state.shape, F32), pltpu.SemaphoreType.DMA((SLOTS // 2,))],
        10**8,
        (wave_table[None], returned),
        [VMEM] * 2,
        "unpack_state",
    )
    return new_state, jnp.transpose(grid, (1, 0, 2))[None]


def solution(mesh):
    placed = (
        P("wave", None, None, None, "lev", None),
        P(),
        P(),
        P(),
        P("wave", None, None),
        P(),
        P(),
        P(),
        P(),
        P(),
        P(),
        P("lev"),
        P(),
    )
    return jax.shard_map(
        per_device,
        mesh=mesh,
        in_specs=placed,
        out_specs=(P("wave", None, None, None, "lev", None), P("lev", None, "wave", None)),
        check_vma=False,
    )
```

```python
import math

import jax
import jax.numpy as jnp
from jax import lax
from jax.experimental import pallas as pl
from jax.experimental.pallas import tpu as pltpu
from jax.sharding import PartitionSpec as P

F32 = jnp.float32
BF16 = jnp.bfloat16
WAVES = 32
LEVS = 8
MW = 256
NTOT = 256
NLAT = 384
NLON = 768
HID = 512
SLOTS = MW // WAVES
BAND = NLAT // WAVES
PAIRS = BAND // 2
LEVELS = 32
FEAT = 64
ROWL = LEVELS // LEVS
time_step = 0.5
nudge_rate = 0.5
diffusion = 0.5

VMEM = pl.BlockSpec(memory_space=pltpu.VMEM)
HBM = pl.BlockSpec(memory_space=pltpu.HBM)


def call(body, outs, scratch, flops, operands, specs, name):
    operands = [
        pltpu.with_memory_space_constraint(o, pltpu.HBM) if spec is HBM else o
        for o, spec in zip(operands, specs)
    ]
    return pl.pallas_call(
        body,
        out_shape=outs,
        in_specs=specs,
        out_specs=jax.tree.map(lambda o: HBM if isinstance(o, pl.MemoryRef) else VMEM, outs),
        scratch_shapes=scratch,
        compiler_params=pltpu.CompilerParams(vmem_limit_bytes=40 * 2**20),
        cost_estimate=pl.CostEstimate(flops=flops, bytes_accessed=2 * 10**6, transcendentals=0),
        name=name,
    )(*operands)


def out(shape, dtype):
    return jax.ShapeDtypeStruct(shape, dtype)


def own_waves(waves_ref):
    lane = lax.broadcasted_iota(jnp.int32, (1, MW), 1)
    row = waves_ref[...].astype(F32)
    first = lax.axis_index("wave") * SLOTS
    return [
        jnp.sum(jnp.where(lane == first + 2 * q, row, 0.0)).astype(jnp.int32)
        for q in range(SLOTS // 2)
    ]


def fold(first, second, q, m, extra):
    lane = lax.broadcasted_iota(jnp.int32, first.shape, 1)
    turned = pltpu.roll(second, m, axis=1)
    block = lax.broadcasted_iota(jnp.int32, extra.shape, 1)
    extra = jnp.where(block == q, pltpu.roll(turned[:, 128:], q + 1, axis=1), extra)
    return jnp.where(lane >= m, first, turned), extra


def unfold(both, extra, q, m):
    lane = lax.broadcasted_iota(jnp.int32, both.shape, 1)
    block = lax.broadcasted_iota(jnp.int32, extra.shape, 1)
    last = jnp.where(block == 127, pltpu.roll(extra, 127 - q, axis=1), both[:, 128:])
    turned = jnp.concatenate([both[:, :128], last], axis=1)
    turned = pltpu.roll(turned, (NTOT - m) & (NTOT - 1), axis=1)
    return jnp.where(lane >= m, both, 0.0), jnp.where(lane >= NTOT - 1 - m, turned, 0.0)


def pack_state(
    waves_hbm, target_hbm, state_hbm, send_ref, rows_ref, state_ref, waves_ref, target_ref, sems, small_sems
):
    copies = [
        pltpu.make_async_copy(state_hbm.at[half], state_ref.at[half], sems.at[i])
        for i, half in enumerate((pl.ds(0, SLOTS // 2), pl.ds(SLOTS // 2, SLOTS // 2)))
    ]
    waves_copy = pltpu.make_async_copy(waves_hbm, waves_ref, small_sems.at[0])
    target_copy = pltpu.make_async_copy(target_hbm, target_ref, small_sems.at[1])
    for copy in (*copies, waves_copy, target_copy):
        copy.start()
    target_copy.wait()
    waves_copy.wait()
    first = lax.axis_index("wave") * SLOTS
    lane = lax.broadcasted_iota(jnp.int32, (16, 128), 1)
    row = lax.broadcasted_iota(jnp.int32, (16, 128), 0)
    rider = jnp.zeros((16, 128), F32)
    for i in range(ROWL):
        rider = jnp.where((lane == SLOTS // 2) & (row == i), target_ref[i], rider)
    extra = jnp.concatenate([rider] * LEVS, axis=0)
    for q in range(SLOTS // 2):
        if q % 2 == 0:
            copies[q // 2].wait()
        for j in (2 * q, 2 * q + 1):
            for e in range(LEVS):
                for c in range(2):
                    rows_ref[j, e, c * 8 : c * 8 + 8, :] = state_ref[j, c, e].reshape(8, NTOT)
        flat = [rows_ref[j].reshape(LEVS * 16, NTOT) for j in (2 * q, 2 * q + 1)]
        both, extra = fold(*flat, q, waves_ref[first + 2 * q], extra)
        send_ref[:, :, q * NTOT : (q + 1) * NTOT] = both.astype(BF16).reshape(LEVS, 16, NTOT)
    send_ref[:, :, 4 * NTOT :] = extra.astype(BF16).reshape(LEVS, 16, 128)


def sine_of(q):
    a = q * (2.0 * math.pi / NLON)
    b = a * a
    total = jnp.full_like(b, -2.5052108e-8)
    for factor in (2.7557319e-6, -1.9841270e-4, 8.3333333e-3, -1.6666667e-1, 1.0):
        total = total * b + factor
    return total * a


def prepare(
    lats_hbm, weights_hbm, lat_ref, weight_ref, waves_ref, legendre_hbm, coupling_hbm, w_in_ref, b_in_ref, w_lat_ref, w_mid_ref,
    b_mid_ref, band_ref, const_ref, cos_t_hbm, sin_t_hbm, cos_hbm, sin_hbm, first_hbm, mid_hbm, bias_hbm, scale_hbm,
    by_level_hbm, hot_ref, cos_t_ref, sin_t_ref, cos_ref, sin_ref, first_ref, mid_ref, bias_ref, scale_ref, by_level_ref, legendre_ref, lats_ref,
    weights_ref, coupling_ref, sems, in_sems,
):
    pairs = (
        (cos_t_ref, cos_t_hbm),
        (sin_t_ref, sin_t_hbm),
        (cos_ref, cos_hbm),
        (sin_ref, sin_hbm),
        (first_ref, first_hbm),
        (mid_ref, mid_hbm),
        (bias_ref, bias_hbm),
        (scale_ref, scale_hbm),
        (by_level_ref, by_level_hbm),
    )
    copies = [pltpu.make_async_copy(a, b, sems.at[i]) for i, (a, b) in enumerate(pairs)]
    legendre_copy = pltpu.make_async_copy(legendre_hbm, legendre_ref, in_sems.at[0])
    lats_copy = pltpu.make_async_copy(lats_hbm, lats_ref, in_sems.at[1])
    weights_copy = pltpu.make_async_copy(weights_hbm, weights_ref, in_sems.at[2])
    coupling_copies = [
        pltpu.make_async_copy(
            coupling_hbm.at[:, pl.ds(i * 128, 128)], coupling_ref.at[i], in_sems.at[3 + i]
        )
        for i in range(2)
    ]
    for copy in (lats_copy, weights_copy, legendre_copy, *coupling_copies):
        copy.start()
    x = lax.broadcasted_iota(jnp.int32, (NLON, MW), 0)
    product = (x * waves_ref[...]).astype(F32)
    phase = product - NLON * jnp.floor(product * (1.0 / NLON) + 0.5)
    size = jnp.abs(phase)
    cosine = sine_of(NLON // 4 - size)
    sine = sine_of(jnp.where(size > NLON // 4, jnp.where(phase > 0, 1.0, -1.0) * (NLON // 2) - phase, phase))
    sine = -sine
    cos_t_ref[...] = (cosine * MW**-0.5).astype(BF16)
    copies[0].start()
    sin_t_ref[...] = (sine * MW**-0.5).astype(BF16)
    copies[1].start()
    cos_ref[...] = cosine.astype(BF16).T
    copies[2].start()
    sin_ref[...] = sine.astype(BF16).T
    copies[3].start()
    first_ref[...] = jnp.zeros_like(first_ref)
    half_in = (w_in_ref[...].astype(F32) * 0.5).astype(BF16)
    first_ref[0, :FEAT, :] = half_in
    first_ref[1, FEAT:, :] = half_in
    copies[4].start()
    mid_ref[...] = (w_mid_ref[...].astype(F32) * 0.5).astype(BF16)
    copies[5].start()
    lane = lax.broadcasted_iota(jnp.int32, (1, BAND * FEAT), 1)
    scale = jnp.zeros((1, BAND * FEAT), F32)
    own = lax.axis_index("wave") * BAND
    lats_copy.wait()
    weights_copy.wait()
    for b in range(BAND):
        t = lats_ref[own + b]
        here = (lane >= b * FEAT) & (lane < (b + 1) * FEAT)
        scale = jnp.where(here, weights_ref[t] * ((2.0 * MW) ** 0.5 / NLON), scale)
        at = jnp.full((1, HID), t, jnp.int32).astype(F32)
        coslat = jnp.sin((at + 0.5) * (math.pi / NLAT))
        bias_ref[b : b + 1, :] = 0.5 * (b_in_ref[...] + coslat * w_lat_ref[...])
    bias_ref[BAND : BAND + 1, :] = 0.5 * b_mid_ref[...]
    copies[6].start()
    scale_ref[...] = scale
    copies[7].start()

    for i in range(2):
        coupling_copies[i].wait()
        for k in range(LEVELS):
            by_level_ref[k, :, i * 128 : (i + 1) * 128] = coupling_ref[
                i, pl.ds(k, LEVELS, stride=LEVELS), :
            ]
    copies[8].start()

    t = lax.broadcasted_iota(jnp.int32, (NLAT, NLAT), 0)
    hot = (t == lat_ref[...]).astype(F32).T
    for i in range(NLAT // 128):
        hot_ref[i] = hot[:, i * 128 : (i + 1) * 128]
    pick = []
    for parity in range(2):
        parts = [
            jnp.concatenate(
                [hot_ref[i, pl.ds(2 * p + parity, WAVES, stride=BAND), :] for p in range(PAIRS)], axis=0
            )
            for i in range(NLAT // 128)
        ]
        pick.append(jnp.concatenate(parts, axis=1).astype(BF16))
    weight = weight_ref[...]
    high = weight.astype(BF16)
    low = (weight - high.astype(F32)).astype(BF16)
    row = lax.broadcasted_iota(jnp.int32, (16, NLAT), 0)
    both = jnp.where(row == 0, high.astype(F32), jnp.where(row == 1, low.astype(F32), 0.0))
    both = both.astype(BF16)
    legendre_copy.wait()
    for j in range(SLOTS):
        block = legendre_ref[j]
        for parity in range(2):
            band_ref[j, :, parity * NTOT : (parity + 1) * NTOT] = jnp.dot(
                pick[parity], block, preferred_element_type=F32
            ).astype(BF16)
        sums = jnp.dot(both, block, preferred_element_type=F32)
        const_ref[j : j + 1, :] = jnp.sum(sums, axis=0, keepdims=True)
    for copy in copies:
        copy.wait()


def to_fourier(
    waves_ref, recv_ref, band_ref, fourier_ref, state_ref, target_ref, rows_ref, both_ref, total_ref
):
    waves = own_waves(waves_ref)
    both_ref[...] = jnp.zeros_like(both_ref)
    extra = recv_ref[:, :, 4 * NTOT :].astype(F32)
    for src in range(LEVS):
        at = src * ROWL
        target_ref[at : at + ROWL, :] = jnp.broadcast_to(
            extra[src, :ROWL, SLOTS // 2 : SLOTS // 2 + 1], (ROWL, 128)
        )
    extra = extra.reshape(LEVS * 16, 128)
    for j in range(SLOTS):
        k = j % 2
        q = j // 2
        if k == 0:
            both = recv_ref[:, :, q * NTOT : (q + 1) * NTOT].astype(F32).reshape(LEVS * 16, NTOT)
            split = unfold(both, extra, q, waves[q])
        for src in range(LEVS):
            block = split[k][src * 16 : (src + 1) * 16]
            for c in range(2):
                for f in range(2):
                    at = f * LEVELS + src * ROWL
                    rows_ref[k, c, at : at + 4, :] = block[c * 8 + f * 4 : c * 8 + f * 4 + 4, :]
        for c in range(2):
            part = rows_ref[k, c].astype(BF16)
            state_ref[j, c] = part
            both_ref[k, c * 128 : c * 128 + 64, :NTOT] = part
            both_ref[k, c * 128 + 64 : c * 128 + 128, NTOT:] = part
        sums = lax.dot_general(
            band_ref[j], both_ref[k], (((1,), (1,)), ((), ())), preferred_element_type=F32
        )
        for c in range(2):
            for p in range(PAIRS):
                total_ref[c * PAIRS + p, pl.ds(j, WAVES, stride=SLOTS), :] = sums[
                    p * WAVES : (p + 1) * WAVES, c * 128 : (c + 1) * 128
                ]
    for i in range(2 * PAIRS):
        fourier_ref[:, i * 128 : (i + 1) * 128] = total_ref[i].astype(BF16)


def half_silu(u):
    return (u + u * jnp.tanh(u)).astype(BF16)


def dot_lanes(a, b):
    return lax.dot_general(a, b, (((1,), (1,)), ((), ())), preferred_element_type=F32)


def columns(
    coef_ref, cos_t_ref, sin_t_ref, first_ref, bias_ref, mid_ref, last_ref, cos_ref, sin_ref, scale_ref,
    tendw_ref, grid_hbm, values_ref, grid_ref, hidden_ref,
    grid_sems,
):
    def grid_copy(p):
        rows = pl.ds(2 * p, 2)
        return pltpu.make_async_copy(grid_ref.at[rows], grid_hbm.at[rows], grid_sems.at[p])

    half = BAND * FEAT
    values = jnp.dot(cos_t_ref[...], coef_ref[:, :half], preferred_element_type=F32)
    values += jnp.dot(sin_t_ref[...], coef_ref[:, half:], preferred_element_type=F32)
    for p in range(PAIRS):
        values_ref[p] = values[:, p * 128 : (p + 1) * 128].astype(BF16)

    for p in range(PAIRS):
        for q in range(2):
            hidden = jnp.dot(values_ref[p], first_ref[q], preferred_element_type=F32)
            hidden_ref[q, 0] = half_silu(hidden + bias_ref[2 * p + q : 2 * p + q + 1, :])
            hidden = jnp.dot(hidden_ref[q, 0], mid_ref[...], preferred_element_type=F32)
            hidden_ref[q, 1] = half_silu(hidden + bias_ref[BAND : BAND + 1, :])
            grid_ref[2 * p + q] = dot_lanes(last_ref[...], hidden_ref[q, 1]).astype(BF16)
        grid_copy(p).start()
    tend = grid_ref[...].reshape(half, NLON)
    scale = scale_ref[...]
    for c, table in enumerate((cos_ref, sin_ref)):
        tendw_ref[:, c * half : (c + 1) * half] = (dot_lanes(table[...], tend) * scale).astype(BF16)
    for p in range(PAIRS):
        grid_copy(p).wait()


def to_spectral(
    waves_ref, recv_ref, band_ref, state_ref, const_ref, weight_ref, target_ref, coupling_ref,
    send_ref, wide_ref, temp_ref, rows_ref, low_ref,
):
    waves = own_waves(waves_ref)
    for i in range(2 * PAIRS):
        wide_ref[i] = recv_ref[:, i * 128 : (i + 1) * 128].astype(F32)
    target = target_ref[:, :1]
    weight_total = jnp.sum(weight_ref[...], axis=1, keepdims=True)
    degree = lax.broadcasted_iota(jnp.int32, (1, NTOT), 1)
    shrink = 1.0 / (1.0 + diffusion * (degree * (degree + 1)).astype(F32) / (NTOT * NTOT))
    for j in range(SLOTS):
        m = waves[j // 2] if j % 2 == 0 else MW - 1 - waves[j // 2]
        live = (degree >= m).astype(F32)
        is_zero = (jnp.full((1, NTOT), m, jnp.int32) == 0).astype(F32)
        block = jnp.concatenate(
            [
                jnp.concatenate(
                    [wide_ref[c * PAIRS + p, pl.ds(j, WAVES, stride=SLOTS), :] for c in range(2)],
                    axis=1,
                )
                for p in range(PAIRS)
            ],
            axis=0,
        )
        parts = block.astype(BF16).T
        tend_sum = jnp.sum(parts[:128].astype(F32), axis=1, keepdims=True)
        even = jnp.concatenate([parts[:64], parts[128:192]], axis=0)
        odd = jnp.concatenate([parts[64:128], parts[192:]], axis=0)
        spec = jnp.dot(even, band_ref[j, :, :NTOT], preferred_element_type=F32)
        spec += jnp.dot(odd, band_ref[j, :, NTOT:], preferred_element_type=F32)
        const = const_ref[j : j + 1, :]
        for c in range(2):
            old = state_ref[j, c].astype(F32)
            old_temp, old_hum = old[:LEVELS], old[LEVELS:]
            temp = spec[c * 64 : c * 64 + 32]
            hum = spec[c * 64 + 32 : c * 64 + 64]
            if c == 0:
                mean = jnp.sum(old_temp * const, axis=1, keepdims=True)
                mean += time_step * (tend_sum[:32] + tend_sum[64:96])
                nudge = nudge_rate * (target - mean / weight_total)
                temp = temp + nudge * (const * is_zero)
            temp_ref[j * 2 + c] = (old_temp + time_step * temp) * live
            hum = (old_hum + time_step * hum) * (live * shrink)
            for d in range(LEVS):
                rows_ref[j, d, c * 8 + 4 : c * 8 + 8, :] = hum[d * 4 : d * 4 + 4]
    for i in range(SLOTS):
        at = i // 2 * 4 + i % 2
        low_ref[i] = temp_ref[at, :, :128] + temp_ref[at + 2, :, :128]
    group = 4
    for g in range(6):
        lanes = slice(0, 128) if g >= 4 else slice(128, NTOT)
        totals = [0.0] * group
        for k in range(LEVELS):
            matrix = coupling_ref[k, :, lanes]
            for i in range(group):
                if g >= 4:
                    temp = low_ref[(g - 4) * group + i, k : k + 1, :]
                else:
                    temp = temp_ref[g * group + i, k : k + 1, lanes]
                totals[i] = totals[i] + matrix * temp
        for i in range(group):
            if g >= 4:
                q, c = divmod((g - 4) * group + i, 2)
                low = jnp.full((LEVELS, 128), waves[q], jnp.int32) < 128
                parts = [
                    (2 * q, jnp.where(low, totals[i], 0.0)),
                    (2 * q + 1, jnp.where(low, 0.0, totals[i])),
                ]
            else:
                j, c = divmod(g * group + i, 2)
                parts = [(j, totals[i])]
            for j, part in parts:
                for d in range(LEVS):
                    rows_ref[j, d, c * 8 : c * 8 + 4, lanes] = part[d * 4 : d * 4 + 4]
    extra = jnp.zeros((LEVS * 16, 128), F32)
    for q in range(SLOTS // 2):
        flat = [rows_ref[j].reshape(LEVS * 16, NTOT) for j in (2 * q, 2 * q + 1)]
        both, extra = fold(*flat, q, waves[q], extra)
        send_ref[:, :, q * NTOT : (q + 1) * NTOT] = both.astype(BF16).reshape(LEVS, 16, NTOT)
    send_ref[:, :, 4 * NTOT :] = extra.astype(BF16).reshape(LEVS, 16, 128)


def unpack_state(waves_ref, recv_ref, state_hbm, state_ref, sems):
    copies = [
        pltpu.make_async_copy(
            state_ref.at[pl.ds(2 * q, 2)], state_hbm.at[pl.ds(2 * q, 2)], sems.at[q]
        )
        for q in range(SLOTS // 2)
    ]
    waves = own_waves(waves_ref)
    extra = recv_ref[:, :, 4 * NTOT :].astype(F32).reshape(LEVS * 16, 128)
    for q in range(SLOTS // 2):
        both = recv_ref[:, :, q * NTOT : (q + 1) * NTOT].astype(F32).reshape(LEVS * 16, NTOT)
        split = unfold(both, extra, q, waves[q])
        for k in range(2):
            for e in range(LEVS):
                for c in range(2):
                    for f in range(2):
                        at = e * 16 + c * 8 + f * 4
                        state_ref[2 * q + k, c, e, f] = split[k][at : at + 4, :]
        copies[q].start()
    for copy in copies:
        copy.wait()


def per_device(
    state,
    wave_table,
    lat_table,
    lat_weight,
    legendre,
    w_in,
    b_in,
    w_lat,
    w_mid,
    b_mid,
    w_out,
    target,
    coupling,
):
    message = (LEVS, 16, SLOTS // 2 * NTOT + 128)
    rows = (SLOTS, LEVS, 16, NTOT)
    sent = call(
        pack_state,
        out(message, BF16),
        [
            pltpu.VMEM(rows, F32),
            pltpu.VMEM(state.shape, F32),
            pltpu.SMEM((MW,), jnp.int32),
            pltpu.SMEM((ROWL,), F32),
            pltpu.SemaphoreType.DMA((2,)),
            pltpu.SemaphoreType.DMA((2,)),
        ],
        10**8,
        (wave_table, target, state),
        [HBM] * 3,
        "pack_state",
    )
    members = lax.all_to_all(sent, "lev", 0, 0, tiled=True)
    table, turned, weights = (NLON, MW), (MW, NLON), (2, 2 * FEAT, HID)
    made = [
        (table, BF16),
        (table, BF16),
        (turned, BF16),
        (turned, BF16),
        (weights, BF16),
        ((HID, HID), BF16),
        ((16, HID), F32),
        ((1, BAND * FEAT), F32),
        ((LEVELS, LEVELS, NTOT), F32),
    ]
    band, const, cos_t, sin_t, cos, sin, first, mid, bias, scale, by_level = call(
        prepare,
        (
            out((SLOTS, PAIRS * WAVES, 2 * NTOT), BF16),
            out((SLOTS, NTOT), F32),
            *(pltpu.HBM(*m) for m in made),
        ),
        [
            pltpu.VMEM((NLAT // 128, NLAT, 128), F32),
            *(pltpu.VMEM(*m) for m in made),
            pltpu.VMEM(legendre.shape, BF16),
            pltpu.SMEM((NLAT,), jnp.int32),
            pltpu.SMEM((NLAT,), F32),
            pltpu.VMEM((2, LEVELS * LEVELS, 128), F32),
            pltpu.SemaphoreType.DMA((len(made),)),
            pltpu.SemaphoreType.DMA((5,)),
        ],
        6 * 10**9,
        (
            lat_table,
            lat_weight,
            lat_table[None],
            lat_weight[None],
            wave_table[None],
            legendre,
            jnp.transpose(coupling, (1, 2, 0)).reshape(LEVELS * LEVELS, NTOT),
            w_in,
            b_in[None],
            w_lat[None],
            w_mid,
            b_mid[None],
        ),
        [HBM] * 2 + [VMEM] * 3 + [HBM] * 2 + [VMEM] * 5,
        "prepare",
    )
    fourier, state_bf, target_all = call(
        to_fourier,
        (
            out((MW, 2 * BAND * FEAT), BF16),
            out((SLOTS, 2, FEAT, NTOT), BF16),
            out((LEVELS, 128), F32),
        ),
        [
            pltpu.VMEM((2, 2, FEAT, NTOT), F32),
            pltpu.VMEM((2, NTOT, 2 * NTOT), BF16),
            pltpu.VMEM((2 * PAIRS, MW, 128), F32),
        ],
        10**9,
        (wave_table[None], members, band),
        [VMEM] * 3,
        "to_fourier",
    )
    coef = lax.all_to_all(fourier, "wave", 0, 0, tiled=True)
    tendw, grid = call(
        columns,
        (
            out((MW, 2 * BAND * FEAT), BF16),
            pltpu.HBM((BAND, FEAT, NLON), BF16),
        ),
        [
            pltpu.VMEM((PAIRS, NLON, 128), BF16),
            pltpu.VMEM((BAND, FEAT, NLON), BF16),
            pltpu.VMEM((2, 2, NLON, HID), BF16),
            pltpu.SemaphoreType.DMA((PAIRS,)),
        ],
        10**10,
        (coef, cos_t, sin_t, first, bias, mid, w_out.T, cos, sin, scale),
        [VMEM] * 10,
        "columns",
    )
    back = lax.all_to_all(tendw, "wave", 0, 0, tiled=True)
    moved = call(
        to_spectral,
        out(message, BF16),
        [
            pltpu.VMEM((2 * PAIRS, MW, 128), F32),
            pltpu.VMEM((2 * SLOTS, LEVELS, NTOT), F32),
            pltpu.VMEM(rows, F32),
            pltpu.VMEM((SLOTS, LEVELS, 128), F32),
        ],
        10**9,
        (
            wave_table[None],
            back,
            band,
            state_bf,
            const,
            lat_weight[None],
            target_all,
            by_level,
        ),
        [VMEM] * 8,
        "to_spectral",
    )
    returned = lax.all_to_all(moved, "lev", 0, 0, tiled=True)
    new_state = call(
        unpack_state,
        pltpu.HBM(state.shape, F32),
        [pltpu.VMEM(state.shape, F32), pltpu.SemaphoreType.DMA((SLOTS // 2,))],
        10**8,
        (wave_table[None], returned),
        [VMEM] * 2,
        "unpack_state",
    )
    return new_state, jnp.transpose(grid, (1, 0, 2))[None]


def solution(mesh):
    placed = (
        P("wave", None, None, None, "lev", None),
        P(),
        P(),
        P(),
        P("wave", None, None),
        P(),
        P(),
        P(),
        P(),
        P(),
        P(),
        P("lev"),
        P(),
    )
    return jax.shard_map(
        per_device,
        mesh=mesh,
        in_specs=placed,
        out_specs=(P("wave", None, None, None, "lev", None), P("lev", None, "wave", None)),
        check_vma=False,
    )
```
